128 devices in a mesh: dp: 8 (over x_lo, z), vocab: 16 (over y, x_hi, core).
Axes of the slice: x: 4 (x_hi: 2, x_lo: 2; x = x_hi * 2 + x_lo), y: 4, z: 4, core: 2. Of those that a mesh axis runs over, the one named last changes fastest.
Arguments:
- student_hidden: bfloat16 [512, 5120], P('dp'), may hold values from -64 to 64
- student_weight: bfloat16 [81920, 5120], P(('dp', 'vocab')), may hold values from -12 to 12
- teacher_hidden: bfloat16 [512, 4096], P('dp'), may hold values from -64 to 64
- teacher_weight: bfloat16 [81920, 4096], P(('dp', 'vocab')), may hold values from -12 to 12
- token_ids: int32 [512], replicated, may hold values from 0 to 81919
- group_ids: int32 [512], replicated, may hold values from 0 to 15, never falling along the last dimension, each value on 1 to 64 neighbouring positions
- response_mask: int32 [512], replicated, may hold values 0 or 1
Outputs:
- kl_tok: float32 [512], P('dp')
- logp_tok: float32 [512], P('dp')
- grad_hidden: bfloat16 [512, 5120], P('dp')
- grad_weight: bfloat16 [81920, 5120], P(('dp', 'vocab'))
The draws below stay inside these ranges and needn't reach their ends.
All inputs are finite; a program needn't handle non-finite values.
Results may differ from the reference program's by a relative error of at most 0.006.
Values may be sent and summed in bfloat16 or wider, within the bound.
No kernel may reach another device: no remote copies, remote signals or barrier semaphores. Data moves between devices by JAX's collectives and lax.ppermute only.
A program may use at most 128 MiB of HBM per device.

```python
import math
import jax
import jax.numpy as jnp
import numpy as np

DS = 5120
DT = 4096
V = 81920
SPAN = 32
TOKENS = 512
GROUPS = 16


def noise_rows(key, count, width):
    return jnp.clip(jax.random.normal(key, (count, width), jnp.float32), -4.0, 4.0)


def draw_student_hidden(key, part):
    key = jax.random.fold_in(key, 1)
    key_noise, key_scale = jax.random.split(key)
    noise = noise_rows(key_noise, TOKENS, DS)
    scale = jnp.exp(jax.random.uniform(key_scale, (TOKENS, 1), jnp.float32, 0.0, math.log(10.0)))
    values = noise * scale
    return values.astype(jnp.bfloat16)


def draw_teacher_hidden(key, part):
    key = jax.random.fold_in(key, 3)
    key_noise, key_scale = jax.random.split(key)
    noise = noise_rows(key_noise, TOKENS, DT)
    scale = jnp.exp(jax.random.uniform(key_scale, (TOKENS, 1), jnp.float32, 0.0, math.log(10.0)))
    values = noise * scale
    return values.astype(jnp.bfloat16)


def draw_student_weight(key, part):
    key = jax.random.fold_in(key, 2)
    key_noise, key_scale = jax.random.split(key, 2)
    noise = noise_rows(key_noise, V, DS) / math.sqrt(DS)
    scale = jnp.exp(jax.random.uniform(key_scale, (V, 1), jnp.float32, 0.0, math.log(3.0)))
    values = noise * scale
    return values.astype(jnp.bfloat16)


def draw_teacher_weight(key, part):
    key = jax.random.fold_in(key, 4)
    key_noise, key_scale = jax.random.split(key, 2)
    noise = noise_rows(key_noise, V, DT) / math.sqrt(DT)
    scale = jnp.exp(jax.random.uniform(key_scale, (V, 1), jnp.float32, 0.0, math.log(3.0)))
    values = noise * scale
    return values.astype(jnp.bfloat16)


def touch_ends(result, own_key, smallest, largest):
    longest = result.shape.index(max(result.shape))
    spots = []
    for shift in (0, 1):
        where = [jax.random.randint(jax.random.fold_in(own_key, axis), (), 0, length) for axis, length in enumerate(result.shape)]
        where[longest] = (where[longest] + shift) % result.shape[longest]
        spots.append(tuple(where))
    return result.at[spots[0]].set(smallest).at[spots[1]].set(largest)


def length_profile(number_of, total, bound, skew):
    weights = [(1 << 20) // math.isqrt(standing ** skew) + 1 for standing in range(2, number_of + 1)]
    rest, given = total - bound - (number_of - 1), [1] * (number_of - 1)
    while rest > 0:
        candidates = [i for i in range(number_of - 1) if given[i] < bound]
        whole, left = sum([weights[i] for i in candidates]), rest
        for i in candidates:
            addition = min(bound - given[i], max(1, left * weights[i] // whole), rest)
            given[i] = given[i] + addition
            rest = rest - addition
    return np.array([bound] + given)


def uneven(key, count, total, bound, lean):
    if count == 2:
        one = jax.random.randint(key, (), max(1, total - bound), min(bound, total - 1) + 1)
        return jnp.stack([one, total - one])
    sizes = jnp.asarray(length_profile(count, total, bound, lean), jnp.int32)
    couples = (count - 1) // 2
    giver, taker = sizes[1:1 + 2 * couples:2], sizes[2:2 + 2 * couples:2]
    margin = jnp.minimum(giver - 1, bound - taker)
    passed = jax.random.randint(jax.random.fold_in(key, 1), (couples,), 0, 1 << 20) % (margin + 1)
    sizes = sizes.at[1:1 + 2 * couples:2].set(giver - passed).at[2:2 + 2 * couples:2].set(taker + passed)
    return sizes[jax.random.permutation(jax.random.fold_in(key, 2), count)]


def setup_inputs(seed: int = 0) -> dict:
    keys = jax.random.split(jax.random.key(seed), 8)
    student_hidden = draw_student_hidden(jax.random.fold_in(keys[7], 71), 0)
    student_weight = draw_student_weight(jax.random.fold_in(keys[7], 71), 0)
    teacher_hidden = draw_teacher_hidden(jax.random.fold_in(keys[7], 71), 0)
    teacher_weight = draw_teacher_weight(jax.random.fold_in(keys[7], 71), 0)
    token_ids = touch_ends(jax.random.randint(keys[4], (TOKENS,), 0, V), jax.random.fold_in(keys[4], 1), 0, V - 1).astype(jnp.int32)
    group_ids = jnp.searchsorted(jnp.cumsum(uneven(keys[5], GROUPS, TOKENS, 2 * SPAN, 2)), jnp.arange(TOKENS), side="right").astype(jnp.int32)
    response_mask = touch_ends((jax.random.randint(keys[6], (TOKENS,), 0, 4) < 3).astype(jnp.int32), jax.random.fold_in(keys[6], 1), 0, 1)
    return dict(student_hidden=student_hidden, student_weight=student_weight, teacher_hidden=teacher_hidden, teacher_weight=teacher_weight, token_ids=token_ids, group_ids=group_ids, response_mask=response_mask)


def log_sum(logits):
    top = jnp.max(logits, axis=1)
    total = jnp.sum(jnp.exp(logits - top[:, None]), axis=1)
    return top + jnp.log(total)


def reference(student_hidden, student_weight, teacher_hidden, teacher_weight, token_ids, group_ids, response_mask):
    student_logits = jnp.einsum("td,vd->tv", student_hidden, student_weight, preferred_element_type=jnp.float32)
    teacher_logits = jnp.einsum("td,vd->tv", teacher_hidden, teacher_weight, preferred_element_type=jnp.float32)
    log_total_s = log_sum(student_logits)
    log_total_t = log_sum(teacher_logits)
    prob_s = jnp.exp(student_logits - log_total_s[:, None])
    prob_t = jnp.exp(teacher_logits - log_total_t[:, None])
    kl_tok = jnp.sum(prob_t * (teacher_logits - student_logits), axis=1) - log_total_t + log_total_s
    picked = jnp.take_along_axis(student_logits, token_ids[:, None].astype(jnp.int32), axis=1)[:, 0]
    logp_tok = picked - log_total_s
    same_group = group_ids[:, None] == group_ids[None, :]
    lengths = jnp.sum(same_group.astype(jnp.float32), axis=1)
    token_weight = response_mask.astype(jnp.float32) * SPAN / lengths
    grad_logits = (token_weight[:, None] * (prob_s - prob_t)).astype(jnp.bfloat16)
    grad_hidden = jnp.dot(grad_logits, student_weight, preferred_element_type=jnp.float32).astype(jnp.bfloat16)
    grad_weight = jnp.einsum("tv,td->vd", grad_logits, student_hidden, preferred_element_type=jnp.float32).astype(jnp.bfloat16)
    return kl_tok, logp_tok, grad_hidden, grad_weight
```

```python
import jax
import jax.numpy as jnp
from jax import lax
from jax.sharding import PartitionSpec as P

SPAN = 32
BOTH = ("dp", "vocab")
F32 = jnp.float32
BF16 = jnp.bfloat16


def coordinates(device):
    dp, vocab = divmod(device, 16)
    x_lo, z = divmod(dp, 4)
    y, rest = divmod(vocab, 4)
    x_hi, core = divmod(rest, 2)
    return x_hi * 2 + x_lo, y, z, core


def device_at(x, y, z, core):
    x_hi, x_lo = divmod(x % 4, 2)
    return (x_lo * 4 + z % 4) * 16 + (y % 4) * 4 + x_hi * 2 + core


def permutation(move):
    return [(i, device_at(*move(*coordinates(i)))) for i in range(128)]


def way(core):
    return 1 - 2 * core


ALONG_Z = permutation(lambda x, y, z, c: (x, y, z + way(c), c))
ALONG_X = permutation(lambda x, y, z, c: (x + way(c), y, z, c))
OTHER_CORE = permutation(lambda x, y, z, c: (x, y, z, 1 - c))
SAME_CORE = [[i for i in range(128) if i % 2 == c] for c in range(2)]
SAME_TOKENS = [[dp * 16 + v * 2 + c for v in range(8)] for dp in range(8) for c in range(2)]


def send(value, where):
    return lax.ppermute(value, BOTH, where)


def gather_tokens(own, core):
    half = own.shape[0] // 2
    near_z = send(own, ALONG_Z)
    near_x = send(lax.dynamic_slice_in_dim(own, core * half, half, 0), ALONG_X)
    far_z = send(lax.dynamic_slice_in_dim(near_z, core * half, half, 0), ALONG_Z)
    near_zx = send(near_z, ALONG_X)
    far_zx = send(far_z, ALONG_X)
    mine = jnp.concatenate([near_z, near_zx, far_z, near_x, far_zx], axis=0)
    return jnp.concatenate([own, mine, send(mine, OTHER_CORE)], axis=0)


def token_order(core, x_lo, z):
    def block(xl, zz):
        return (xl * 4 + jnp.remainder(zz, 4)) * 2

    def arrived(c):
        s = 1 - 2 * c
        near, near_x = block(x_lo, z - s), block(1 - x_lo, z - s)
        return [near, near + 1, near_x, near_x + 1, block(x_lo, z + 2) + c, block(1 - x_lo, z) + c, block(1 - x_lo, z + 2) + c]

    own = block(x_lo, z)
    return jnp.stack([own, own + 1] + arrived(core) + arrived(1 - core))


def shards(
    student_hidden,
    student_weight,
    teacher_hidden,
    teacher_weight,
    token_ids,
    group_ids,
    response_mask,
):
    own_rows = student_hidden.shape[0]
    head_rows, width = student_weight.shape
    tokens = token_ids.shape[0]
    dp, vocab = lax.axis_index("dp"), lax.axis_index("vocab")
    core = vocab % 2
    device_index = dp * 16 + vocab
    half_width = width // 2
    weight_mine = lax.dynamic_slice_in_dim(student_weight, core * half_width, half_width, 1)
    weight_theirs = send(
        lax.dynamic_slice_in_dim(student_weight, (1 - core) * half_width, half_width, 1), OTHER_CORE
    )
    hidden_s = gather_tokens(student_hidden, core)
    hidden_t = gather_tokens(teacher_hidden, core)
    student_logits = jnp.einsum("td,vd->tv", hidden_s, student_weight, preferred_element_type=F32)
    teacher_logits = jnp.einsum("td,vd->tv", hidden_t, teacher_weight, preferred_element_type=F32)

    half = own_rows // 2
    order = token_order(core, dp // 4, dp % 4)
    token_at = (order[:, None] * half + jnp.arange(half, dtype=jnp.int32)[None, :]).reshape(tokens)
    everyone = jnp.arange(tokens, dtype=jnp.int32)
    same = token_at[:, None] == everyone[None, :]

    def to_gathered(value):
        return jnp.sum(jnp.where(same, value[None, :], 0), axis=1)

    def to_tokens(value):
        return jnp.sum(jnp.where(same, value[:, None], 0), axis=0)

    ids = to_gathered(token_ids)
    column = lax.broadcasted_iota(jnp.int32, (1, head_rows), 1) + device_index * head_rows
    picked_local = jnp.sum(jnp.where(ids[:, None] == column, student_logits, 0.0), axis=1)
    top_s = jnp.max(student_logits, axis=1)
    top_t = jnp.max(teacher_logits, axis=1)
    sum_s = jnp.sum(jnp.exp(student_logits - top_s[:, None]), axis=1)
    exp_t = jnp.exp(teacher_logits - top_t[:, None])
    sum_t = jnp.sum(exp_t, axis=1)
    cross_local = jnp.sum(exp_t * (teacher_logits - student_logits), axis=1) / sum_t
    own_stats = jnp.stack(
        [to_tokens(v) for v in (top_s + jnp.log(sum_s), top_t + jnp.log(sum_t), cross_local, picked_local)]
    )
    halves = own_stats.reshape(4, 2, tokens // 2).transpose(1, 0, 2).reshape(1, 2, 4, tokens // 2)
    spread = jnp.broadcast_to(halves, (64, 2, 4, tokens // 2)).reshape(128, 8, tokens // 4)
    every = lax.all_to_all(spread, BOTH, split_axis=0, concat_axis=0, tiled=True)
    every = every.reshape(128, 4, tokens // 2)
    all_s, all_t = every[:, 0], every[:, 1]
    max_s, max_t = jnp.max(all_s, axis=0), jnp.max(all_t, axis=0)
    total_s = max_s + jnp.log(jnp.sum(jnp.exp(all_s - max_s), axis=0))
    total_t = max_t + jnp.log(jnp.sum(jnp.exp(all_t - max_t), axis=0))
    cross = jnp.sum(jnp.exp(all_t - total_t) * every[:, 2], axis=0)
    picked = jnp.sum(every[:, 3], axis=0)
    mine = jnp.stack([total_s, total_t, cross - total_t + total_s, picked - total_s])
    other = send(mine, OTHER_CORE)
    first = core == 0
    log_total_s, log_total_t, kl_all, logp_all = jnp.concatenate(
        [jnp.where(first, mine, other), jnp.where(first, other, mine)], axis=1
    )

    same_group = group_ids[:, None] == group_ids[None, :]
    lengths = jnp.sum(same_group.astype(F32), axis=1)
    token_weight = response_mask.astype(F32) * SPAN / lengths
    prob_s = jnp.exp(student_logits - to_gathered(log_total_s)[:, None])
    prob_t = jnp.exp(teacher_logits - to_gathered(log_total_t)[:, None])
    grad_logits = (to_gathered(token_weight)[:, None] * (prob_s - prob_t)).astype(BF16)

    grad_mine = jnp.einsum("gt,gv->tv", same.astype(BF16), grad_logits, preferred_element_type=F32).astype(BF16)
    grad_theirs = send(grad_mine, OTHER_CORE)
    share = (
        jnp.dot(grad_mine, weight_mine, preferred_element_type=F32)
        + jnp.dot(grad_theirs, weight_theirs, preferred_element_type=F32)
    ).astype(BF16)
    piece = tokens // 64
    parts = lax.all_to_all(
        share.reshape(64, piece, half_width), BOTH, split_axis=0, concat_axis=0, tiled=True, axis_index_groups=SAME_CORE
    )
    summed = jnp.sum(parts.astype(F32), axis=0).astype(BF16)
    columns_mine = lax.all_to_all(
        jnp.broadcast_to(summed[None], (8, piece, half_width)),
        BOTH, split_axis=0, concat_axis=0, tiled=True, axis_index_groups=SAME_TOKENS,
    ).reshape(own_rows, half_width)
    columns_theirs = send(columns_mine, OTHER_CORE)
    grad_hidden = jnp.concatenate(
        [jnp.where(first, columns_mine, columns_theirs), jnp.where(first, columns_theirs, columns_mine)], axis=1
    )
    grad_weight = jnp.einsum("tv,td->vd", grad_logits, hidden_s, preferred_element_type=F32).astype(BF16)
    kl_tok = lax.dynamic_slice_in_dim(kl_all, dp * own_rows, own_rows, 0)
    logp_tok = lax.dynamic_slice_in_dim(logp_all, dp * own_rows, own_rows, 0)
    return (kl_tok, logp_tok, grad_hidden, grad_weight)


def solution(mesh):
    in_specs = (
        P("dp", None),
        P(("dp", "vocab"), None),
        P("dp", None),
        P(("dp", "vocab"), None),
        P(),
        P(),
        P(),
    )
    out_specs = (P("dp"), P("dp"), P("dp", None), P(("dp", "vocab"), None))
    return jax.shard_map(shards, mesh=mesh, in_specs=in_specs, out_specs=out_specs, check_vma=False)
```

```python
import functools

import jax
import jax.numpy as jnp
from jax import lax
from jax.experimental import pallas as pl
from jax.experimental.pallas import tpu as pltpu
from jax.sharding import PartitionSpec as P

SPAN = 32
BOTH = ("dp", "vocab")
F32 = jnp.float32
BF16 = jnp.bfloat16
I32 = jnp.int32
VMEM_BYTES = 63 * 1024 * 1024


def coordinates(device):
    dp, vocab = divmod(device, 16)
    x_lo, z = divmod(dp, 4)
    y, rest = divmod(vocab, 4)
    x_hi, core = divmod(rest, 2)
    return x_hi * 2 + x_lo, y, z, core


def device_at(x, y, z, core):
    x_hi, x_lo = divmod(x % 4, 2)
    return (x_lo * 4 + z % 4) * 16 + (y % 4) * 4 + x_hi * 2 + core


def permutation(move):
    return [(i, device_at(*move(*coordinates(i)))) for i in range(128)]


def way(core):
    return 1 - 2 * core


ALONG_Z = permutation(lambda x, y, z, c: (x, y, z + way(c), c))
ALONG_X = permutation(lambda x, y, z, c: (x + way(c), y, z, c))
ALONG_Y = permutation(lambda x, y, z, c: (x, y + way(c), z, c))
OTHER_CORE = permutation(lambda x, y, z, c: (x, y, z, 1 - c))
SAME_TOKENS = [[dp * 16 + v * 2 + c for v in range(8)] for dp in range(8) for c in range(2)]
SAME_CORE = [[i for i in range(128) if i % 2 == c] for c in range(2)]


def send(value, where):
    return lax.ppermute(value, BOTH, where)


def after(done, then):
    both = lax.optimization_barrier((done, then))
    return both


def swap(blocks):
    return [send(block, OTHER_CORE) for block in blocks]


def gather_tokens(kept, weight_columns):
    near_z, near_x, weight_columns = lax.optimization_barrier((send(kept, ALONG_Z), send(kept, ALONG_X), weight_columns))
    second = [send(near_z, ALONG_X), send(near_z, ALONG_Z), send(near_z, ALONG_Y)] + swap([near_z, near_x])
    near_zx, far_z, rest_z, o_near_z, o_near_x = lax.optimization_barrier(second)
    third = [send(far_z, ALONG_X), send(near_zx, ALONG_Y)] + swap([near_zx, far_z, rest_z])
    far_zx, rest_zx, o_near_zx, o_far_z, o_rest_z = lax.optimization_barrier(third)
    o_rest_zx, o_far_zx, weight_columns = lax.optimization_barrier((*swap([rest_zx, far_zx]), weight_columns))
    mine = [near_z, rest_z, near_x, far_z, near_zx, rest_zx, far_zx]
    theirs = [o_near_z, o_rest_z, o_near_x, o_far_z, o_near_zx, o_rest_zx, o_far_zx]
    return mine + theirs, send(weight_columns, OTHER_CORE)


def first_rows(core, odd, x_lo, z, half):
    def block(xl, zz):
        return (xl * 4 + jnp.remainder(zz, 4)) * 2

    def arrived(c):
        s = 1 - 2 * c
        k = c + odd - 2 * c * odd
        return [
            block(x_lo, z - s) + k,
            block(x_lo, z - s) + 1 - k,
            block(1 - x_lo, z) + k,
            block(x_lo, z + 2) + k,
            block(1 - x_lo, z - s) + k,
            block(1 - x_lo, z - s) + 1 - k,
            block(1 - x_lo, z + 2) + k,
        ]

    return [half * b for b in [block(x_lo, z)] + arrived(core) + arrived(1 - core)]


def start_all(copies):
    for copy in copies:
        copy.start()
    return copies


def wait_all(copies):
    for copy in copies:
        copy.wait()


def half_kernel(scalars, student, teacher, out, here, sems):
    half, width = out.shape[0], student.shape[1]
    rows = pl.ds(pl.multiple_of(scalars[0] * half, half), half)
    loads = [
        pltpu.make_async_copy(student.at[rows], here.at[:, pl.ds(0, width)], sems.at[0]),
        pltpu.make_async_copy(teacher.at[rows], here.at[:, pl.ds(width, teacher.shape[1])], sems.at[1]),
    ]
    wait_all(start_all(loads))
    store = pltpu.make_async_copy(here, out, sems.at[2])
    store.start()
    store.wait()


def place(scalars, own, blocks, columns, hidden, half, sems):
    copies = []
    for i, block in enumerate([own] + [b.at[:, columns] for b in blocks]):
        rows = pl.ds(pl.multiple_of(scalars[i], half), own.shape[0] if i == 0 else half)
        copies.append(pltpu.make_async_copy(block, hidden.at[rows], sems.at[i]))
    return start_all(copies)


def rows_product(weight, hidden, out, at):
    out[at] = lax.dot_general(weight[at], hidden[...], (((1,), (1,)), ((), ())), preferred_element_type=F32)


def logits_kernel(half, scalars, own_s, own_t, *refs):
    blocks = refs[:14]
    weight_s, weight_t, ids, out_s, out_t, stats, out_hidden = refs[14:21]
    hidden_s, hidden_t, here_s, here_t, logits_s, logits_t, spread, place_sems, sems = refs[21:]
    rows = out_s.shape[0] // 2
    width_s, width_t = hidden_s.shape[1], hidden_t.shape[1]
    parts = [slice(i * rows, (i + 1) * rows) for i in range(2)]
    heads = [
        (own_s, pl.ds(0, width_s), weight_s, out_s, hidden_s, here_s, logits_s),
        (own_t, pl.ds(width_s, width_t), weight_t, out_t, hidden_t, here_t, logits_t),
    ]
    placing, loads, stores = [], [], []
    for h, (own, columns, weight, out, hidden, here, logits) in enumerate(heads):
        placing.append(place(scalars, own, blocks, columns, hidden, half, place_sems.at[h]))
        loads.append(
            start_all([pltpu.make_async_copy(weight.at[at], here.at[at], sems.at[h, i]) for i, at in enumerate(parts)])
        )
        stores.append([pltpu.make_async_copy(logits.at[at], out.at[at], sems.at[h, 2 + i]) for i, at in enumerate(parts)])

    def product(h):
        _, _, _, _, hidden, here, logits = heads[h]
        wait_all(placing[h])
        for i, at in enumerate(parts):
            loads[h][i].wait()
            rows_product(here, hidden, logits, at)
            stores[h][i].start()

    tiles = [slice(j * 128, (j + 1) * 128) for j in range(out_s.shape[1] // 128)]

    def put(j, row, value):
        side, k = divmod(j, 2)
        spread[:, side, pl.ds(row * 2 + k, 1), :] = jnp.broadcast_to(value[None], (spread.shape[0], 1, 128))

    product(0)
    keep = pltpu.make_async_copy(hidden_s, out_hidden, sems.at[1, 4])
    keep.start()
    entry = lax.broadcasted_iota(I32, (out_s.shape[0], 128), 0) + scalars[15]
    for j, at in enumerate(tiles):
        s = logits_s[:, at]
        top = jnp.max(s, axis=0, keepdims=True)
        put(j, 0, top + jnp.log(jnp.sum(jnp.exp(s - top), axis=0, keepdims=True)))
        put(j, 3, jnp.sum(jnp.where(ids[:, at] == entry, s, 0.0), axis=0, keepdims=True))
    product(1)
    for j, at in enumerate(tiles):
        t = logits_t[:, at]
        top = jnp.max(t, axis=0, keepdims=True)
        exp_t = jnp.exp(t - top)
        total = jnp.sum(exp_t, axis=0, keepdims=True)
        put(j, 1, top + jnp.log(total))
        put(j, 2, jnp.sum(exp_t * (t - logits_s[:, at]), axis=0, keepdims=True) / total)
    last = pltpu.make_async_copy(spread, stats, sems.at[0, 4])
    last.start()
    wait_all(stores[0])
    wait_all(stores[1])
    last.wait()
    keep.wait()


def combine_kernel(every, out):
    stats = every[...]
    lse = stats[:, 0:4]
    top = jnp.max(lse, axis=0)
    total = top + jnp.log(jnp.sum(jnp.exp(lse - top[None]), axis=0))
    total_s, total_t = total[0:2], total[2:4]
    cross = jnp.sum(jnp.exp(stats[:, 2:4] - total_t[None]) * stats[:, 4:6], axis=0)
    picked = jnp.sum(stats[:, 6:8], axis=0)
    out[0:4] = total
    out[4:6] = cross - total_t + total_s
    out[6:8] = picked - total_s


def share_kernel(
    scalars, mine, other, factor, s_mine, t_mine, s_theirs, t_theirs, weight_mine, weight_theirs, share, out_t,
    small, totals, s_here, t_here, grad, grad_t, weight, part, sems,
):
    rows, width = weight_theirs.shape
    tokens = s_mine.shape[1]
    tile = weight.shape[2]
    steps = width // tile
    count = rows // 128
    figures = start_all(
        [pltpu.make_async_copy(mine, small.at[0], sems.at[4, 2]), pltpu.make_async_copy(other, small.at[1], sems.at[4, 3])]
    )
    logits = []
    for side, (s, t) in enumerate(((s_mine, t_mine), (s_theirs, t_theirs))):
        for j in range(count):
            at, to = pl.ds(j * 128, 128), pl.ds(side * rows + j * 128, 128)
            logits.append(
                start_all(
                    [
                        pltpu.make_async_copy(s.at[at], s_here.at[to], sems.at[side, j]),
                        pltpu.make_async_copy(t.at[at], t_here.at[to], sems.at[2 + side, j]),
                    ]
                )
            )
    waiting = []
    for k in range(steps):
        columns = pl.ds(pl.multiple_of(scalars[0] * width + k * tile, 128), tile)
        waiting.append(
            start_all(
                [
                    pltpu.make_async_copy(weight_mine.at[:, columns], weight.at[k, pl.ds(0, rows)], sems.at[5, k]),
                    pltpu.make_async_copy(
                        weight_theirs.at[:, pl.ds(k * tile, tile)], weight.at[k, pl.ds(rows, rows)], sems.at[6, k]
                    ),
                ]
            )
        )
    first = scalars[0] == 0
    wait_all(figures)
    low, high = jnp.where(first, small[0], small[1]), jnp.where(first, small[1], small[0])
    for j in range(tokens // 128):
        half, k = (low, high)[j // 2], j % 2
        for i in range(2):
            totals[i : i + 1, j * 128 : (j + 1) * 128] = half[2 * i + k : 2 * i + k + 1]
    stores = []
    for i, pair in enumerate(logits):
        wait_all(pair)
        at = slice(i * 128, (i + 1) * 128)
        value = factor[...] * (jnp.exp(s_here[at] - totals[0:1]) - jnp.exp(t_here[at] - totals[1:2]))
        if i < count:
            grad_t[at] = value.astype(BF16)
            stores.append(pltpu.make_async_copy(grad_t.at[pl.ds(i * 128, 128)], out_t.at[pl.ds(i * 128, 128)], sems.at[7, i]))
            stores[-1].start()
        grad[:, at] = value.T.astype(BF16)
    written = 0
    for k in range(steps):
        wait_all(waiting[k])
        product = jnp.dot(grad[...], weight[k], preferred_element_type=F32).astype(BF16)
        for j in range(tile // 256):
            high_at, low_at = divmod(k * tile + j * 256, share.shape[3])
            part[:, high_at, :, pl.ds(low_at, 256)] = product[:, j * 256 : (j + 1) * 256].reshape(share.shape[0], 16, 256)
        while (k + 1) * tile >= (written + 1) * share.shape[3]:
            stores.append(pltpu.make_async_copy(part.at[:, written], share.at[:, written], sems.at[4, written]))
            stores[-1].start()
            written += 1
    wait_all(stores)


def grad_weight_kernel(grad, hidden, out):
    out[...] = jnp.dot(grad[...], hidden[...], preferred_element_type=F32).astype(BF16)


def sum_kernel(parts, out):
    count = parts.shape[0] // 16
    total = jnp.sum(parts[0:count].astype(F32), axis=0)
    for i in range(1, 16):
        total += jnp.sum(parts[count * i : count * (i + 1)].astype(F32), axis=0)
    out[...] = jnp.broadcast_to(total.astype(BF16)[None], out.shape)


def assemble_kernel(scalars, mine, theirs, out):
    width = mine.shape[2]
    first = scalars[0] == 0
    low = jnp.where(first, mine[...], theirs[...])
    high = jnp.where(first, theirs[...], mine[...])
    for core, pieces in enumerate((low, high)):
        for v in range(8):
            column = (core * 2 + v % 2) * width
            out[v // 2 * 16 : v // 2 * 16 + 16, column : column + width] = pieces[v]


IN_VMEM = pl.BlockSpec(memory_space=pltpu.VMEM)
IN_HBM = pl.BlockSpec(memory_space=pltpu.HBM)
IN_SMEM = pl.BlockSpec(memory_space=pltpu.SMEM)


def params(limit=VMEM_BYTES):
    return pltpu.CompilerParams(vmem_limit_bytes=limit)


def shards(
    student_hidden,
    student_weight,
    teacher_hidden,
    teacher_weight,
    token_ids,
    group_ids,
    response_mask,
):
    own_rows = student_hidden.shape[0]
    half = own_rows // 2
    head_rows, width = student_weight.shape
    width_t = teacher_weight.shape[1]
    tokens = token_ids.shape[0]
    dp, vocab = lax.axis_index("dp"), lax.axis_index("vocab")
    core = vocab % 2
    odd = (vocab // 4) % 2
    half_width = width // 2
    scalars = jnp.stack(first_rows(core, odd, dp // 4, dp % 4, half) + [(dp * 16 + vocab) * head_rows]).astype(I32)
    core_scalar = core.astype(I32).reshape(1)

    kept = pl.pallas_call(
        half_kernel,
        in_specs=[IN_SMEM] + [IN_HBM] * 2,
        out_specs=IN_HBM,
        out_shape=jax.ShapeDtypeStruct((half, width + width_t), BF16),
        scratch_shapes=[pltpu.VMEM((half, width + width_t), BF16), pltpu.SemaphoreType.DMA((3,))],
        compiler_params=params(),
    )((core + odd - 2 * core * odd).astype(I32).reshape(1), student_hidden, teacher_hidden)
    blocks, weight_theirs = gather_tokens(
        kept, lax.dynamic_slice_in_dim(student_weight, (1 - core) * half_width, half_width, 1)
    )

    same_group = group_ids[:, None] == group_ids[None, :]
    lengths = jnp.sum(same_group.astype(F32), axis=1)
    token_weight = (response_mask.astype(F32) * SPAN / lengths).reshape(1, tokens)

    student_logits, teacher_logits, stats, hidden = pl.pallas_call(
        functools.partial(logits_kernel, half),
        in_specs=[IN_SMEM] + [IN_HBM] * 18 + [IN_VMEM],
        out_specs=[IN_HBM] * 4,
        out_shape=[
            jax.ShapeDtypeStruct((head_rows, tokens), F32),
            jax.ShapeDtypeStruct((head_rows, tokens), F32),
            jax.ShapeDtypeStruct((64, 2, 8, 128), F32),
            jax.ShapeDtypeStruct((tokens, width), BF16),
        ],
        scratch_shapes=[
            pltpu.VMEM((tokens, width), BF16),
            pltpu.VMEM((tokens, width_t), BF16),
            pltpu.VMEM((head_rows, width), BF16),
            pltpu.VMEM((head_rows, width_t), BF16),
            pltpu.VMEM((head_rows, tokens), F32),
            pltpu.VMEM((head_rows, tokens), F32),
            pltpu.VMEM((64, 2, 8, 128), F32),
            pltpu.SemaphoreType.DMA((2, 15)),
            pltpu.SemaphoreType.DMA((2, 5)),
        ],
        compiler_params=params(),
        cost_estimate=pl.CostEstimate(
            flops=2 * head_rows * tokens * (width + width_t), bytes_accessed=24_000_000, transcendentals=2 * head_rows * tokens
        ),
    )(scalars, student_hidden, teacher_hidden, *blocks, student_weight, teacher_weight, token_ids.reshape(1, tokens))

    stats, (student_logits, teacher_logits) = lax.optimization_barrier((stats, (student_logits, teacher_logits)))
    student_theirs, teacher_theirs = swap([student_logits, teacher_logits])
    every = lax.all_to_all(stats.reshape(128, 8, 128), BOTH, split_axis=0, concat_axis=0, tiled=True)
    mine = pl.pallas_call(
        combine_kernel,
        in_specs=[IN_VMEM],
        out_specs=IN_VMEM,
        out_shape=jax.ShapeDtypeStruct((8, 128), F32),
        compiler_params=params(4 * 1024 * 1024),
    )(every)
    other = send(mine, OTHER_CORE)

    groups, quarter = tokens // 16, half_width // 2
    share, grad_t = pl.pallas_call(
        share_kernel,
        in_specs=[IN_SMEM] + [IN_HBM] * 2 + [IN_VMEM] + [IN_HBM] * 6,
        out_specs=[IN_HBM, IN_HBM],
        out_shape=[
            jax.ShapeDtypeStruct((groups, 2, 16, quarter), BF16),
            jax.ShapeDtypeStruct((head_rows, tokens), BF16),
        ],
        scratch_shapes=[
            pltpu.VMEM((2, 8, 128), F32),
            pltpu.VMEM((8, tokens), F32),
            pltpu.VMEM((2 * head_rows, tokens), F32),
            pltpu.VMEM((2 * head_rows, tokens), F32),
            pltpu.VMEM((tokens, 2 * head_rows), BF16),
            pltpu.VMEM((head_rows, tokens), BF16),
            pltpu.VMEM((half_width // 512, 2 * head_rows, 512), BF16),
            pltpu.VMEM((groups, 2, 16, quarter), BF16),
            pltpu.SemaphoreType.DMA((8, 5)),
        ],
        compiler_params=params(),
        cost_estimate=pl.CostEstimate(flops=2 * head_rows * tokens * width, bytes_accessed=16_000_000, transcendentals=0),
    )(
        core_scalar, mine, other, token_weight, student_logits, teacher_logits, student_theirs, teacher_theirs,
        student_weight, weight_theirs,
    )
    parts = lax.all_to_all(
        share.reshape(64, 16, quarter), BOTH, split_axis=0, concat_axis=0, tiled=True, axis_index_groups=SAME_CORE
    )

    grad_weight = pl.pallas_call(
        grad_weight_kernel,
        grid=(width // 1024,),
        in_specs=[
            pl.BlockSpec((head_rows, tokens), lambda k: (0, 0)),
            pl.BlockSpec((tokens, 1024), lambda k: (0, k)),
        ],
        out_specs=pl.BlockSpec((head_rows, 1024), lambda k: (0, k)),
        out_shape=jax.ShapeDtypeStruct((head_rows, width), BF16),
        compiler_params=params(16 * 1024 * 1024),
        cost_estimate=pl.CostEstimate(flops=2 * head_rows * tokens * width, bytes_accessed=13_000_000, transcendentals=0),
    )(grad_t, hidden)
    low, high = jnp.where(core == 0, mine, other), jnp.where(core == 0, other, mine)
    kl_all = jnp.concatenate([low[4:6], high[4:6]]).reshape(tokens)
    logp_all = jnp.concatenate([low[6:8], high[6:8]]).reshape(tokens)
    kl_tok = lax.dynamic_slice_in_dim(kl_all, dp * own_rows, own_rows, 0)
    logp_tok = lax.dynamic_slice_in_dim(logp_all, dp * own_rows, own_rows, 0)
    parts, grad_weight, kl_tok, logp_tok = lax.optimization_barrier((parts, grad_weight, kl_tok, logp_tok))

    summed = pl.pallas_call(
        sum_kernel,
        in_specs=[IN_VMEM],
        out_specs=IN_VMEM,
        out_shape=jax.ShapeDtypeStruct((8, 16, quarter), BF16),
        compiler_params=params(8 * 1024 * 1024),
    )(parts)
    pieces_mine = lax.all_to_all(
        summed,
        BOTH, split_axis=0, concat_axis=0, tiled=True, axis_index_groups=SAME_TOKENS,
    )
    pieces_theirs = send(pieces_mine, OTHER_CORE)
    grad_hidden = pl.pallas_call(
        assemble_kernel,
        in_specs=[IN_SMEM] + [IN_VMEM] * 2,
        out_specs=IN_VMEM,
        out_shape=jax.ShapeDtypeStruct((own_rows, width), BF16),
        compiler_params=params(8 * 1024 * 1024),
    )(core_scalar, pieces_mine, pieces_theirs)
    return (kl_tok, logp_tok, grad_hidden, grad_weight)


def solution(mesh):
    in_specs = (
        P("dp", None),
        P(("dp", "vocab"), None),
        P("dp", None),
        P(("dp", "vocab"), None),
        P(),
        P(),
        P(),
    )
    out_specs = (P("dp"), P("dp"), P("dp", None), P(("dp", "vocab"), None))
    return jax.shard_map(shards, mesh=mesh, in_specs=in_specs, out_specs=out_specs, check_vma=False)
```

```python
import functools

import jax
import jax.numpy as jnp
from jax import lax
from jax.experimental import pallas as pl
from jax.experimental.pallas import tpu as pltpu
from jax.sharding import PartitionSpec as P

SPAN = 32
BOTH = ("dp", "vocab")
F32 = jnp.float32
BF16 = jnp.bfloat16
I32 = jnp.int32
VMEM_BYTES = 63 * 1024 * 1024


def coordinates(device):
    dp, vocab = divmod(device, 16)
    x_lo, z = divmod(dp, 4)
    y, rest = divmod(vocab, 4)
    x_hi, core = divmod(rest, 2)
    return x_hi * 2 + x_lo, y, z, core


def device_at(x, y, z, core):
    x_hi, x_lo = divmod(x % 4, 2)
    return (x_lo * 4 + z % 4) * 16 + (y % 4) * 4 + x_hi * 2 + core


def permutation(move):
    return [(i, device_at(*move(*coordinates(i)))) for i in range(128)]


def way(core):
    return 1 - 2 * core


ALONG_Z = permutation(lambda x, y, z, c: (x, y, z + way(c), c))
ALONG_X = permutation(lambda x, y, z, c: (x + way(c), y, z, c))
ALONG_Y = permutation(lambda x, y, z, c: (x, y + way(c), z, c))
OTHER_CORE = permutation(lambda x, y, z, c: (x, y, z, 1 - c))
SAME_TOKENS = [[dp * 16 + v * 2 + c for v in range(8)] for dp in range(8) for c in range(2)]
SAME_CORE = [[i for i in range(128) if i % 2 == c] for c in range(2)]


def send(value, where):
    return lax.ppermute(value, BOTH, where)


def after(done, then):
    both = lax.optimization_barrier((done, then))
    return both


def swap(blocks):
    return [send(block, OTHER_CORE) for block in blocks]


def gather_tokens(kept, others):
    near_z, near_x, others = lax.optimization_barrier((send(kept, ALONG_Z), send(kept, ALONG_X), others))
    second = [send(near_z, ALONG_X), send(near_z, ALONG_Z), send(near_z, ALONG_Y)] + swap([near_z, near_x])
    near_zx, far_z, rest_z, o_near_z, o_near_x = lax.optimization_barrier(second)
    third = [send(far_z, ALONG_X), send(near_zx, ALONG_Y)] + swap([near_zx, far_z, rest_z])
    far_zx, rest_zx, o_near_zx, o_far_z, o_rest_z = lax.optimization_barrier(third)
    scalars, core_scalar, token_weight, ids, weight_columns = others
    o_rest_zx, o_far_zx, weight_columns = lax.optimization_barrier((*swap([rest_zx, far_zx]), weight_columns))
    weight_theirs = send(weight_columns, OTHER_CORE)
    mine = [near_z, rest_z, near_x, far_z, near_zx, rest_zx, far_zx]
    theirs = [o_near_z, o_rest_z, o_near_x, o_far_z, o_near_zx, o_rest_zx, o_far_zx]
    return mine + theirs, (scalars, core_scalar, token_weight, ids, weight_theirs)


def first_rows(core, odd, x_lo, z, half):
    def block(xl, zz):
        return (xl * 4 + jnp.remainder(zz, 4)) * 2

    def arrived(c):
        s = 1 - 2 * c
        k = c + odd - 2 * c * odd
        return [
            block(x_lo, z - s) + k,
            block(x_lo, z - s) + 1 - k,
            block(1 - x_lo, z) + k,
            block(x_lo, z + 2) + k,
            block(1 - x_lo, z - s) + k,
            block(1 - x_lo, z - s) + 1 - k,
            block(1 - x_lo, z + 2) + k,
        ]

    return [half * b for b in [block(x_lo, z)] + arrived(core) + arrived(1 - core)]


def start_all(copies):
    for copy in copies:
        copy.start()
    return copies


def wait_all(copies):
    for copy in copies:
        copy.wait()


def half_kernel(scalars, student, teacher, out, here, sems):
    half, width = out.shape[0], student.shape[1]
    rows = pl.ds(pl.multiple_of(scalars[0] * half, half), half)
    loads = [
        pltpu.make_async_copy(student.at[rows], here.at[:, pl.ds(0, width)], sems.at[0]),
        pltpu.make_async_copy(teacher.at[rows], here.at[:, pl.ds(width, teacher.shape[1])], sems.at[1]),
    ]
    wait_all(start_all(loads))
    store = pltpu.make_async_copy(here, out, sems.at[2])
    store.start()
    store.wait()


def place(scalars, own, blocks, columns, hidden, half, sems):
    copies = []
    for i, block in enumerate([own] + [b.at[:, columns] for b in blocks]):
        rows = pl.ds(pl.multiple_of(scalars[i], half), own.shape[0] if i == 0 else half)
        copies.append(pltpu.make_async_copy(block, hidden.at[rows], sems.at[i]))
    return start_all(copies)


def rows_product(weight, hidden, out, at):
    out[at] = lax.dot_general(weight[at], hidden[...], (((1,), (1,)), ((), ())), preferred_element_type=F32)


def logits_kernel(half, scalars, own_s, own_t, *refs):
    blocks = refs[:14]
    weight_s, weight_t, ids, out_s, out_t, stats, out_hidden = refs[14:21]
    hidden_s, hidden_t, here_s, here_t, logits_s, logits_t, place_sems, sems = refs[21:]
    rows = out_s.shape[0] // 2
    width_s, width_t = hidden_s.shape[1], hidden_t.shape[1]
    parts = [slice(i * rows, (i + 1) * rows) for i in range(2)]
    heads = [
        (own_s, pl.ds(0, width_s), weight_s, out_s, hidden_s, here_s, logits_s),
        (own_t, pl.ds(width_s, width_t), weight_t, out_t, hidden_t, here_t, logits_t),
    ]
    placing, loads, stores = [], [], []
    for h, (own, columns, weight, out, hidden, here, logits) in enumerate(heads):
        loads.append([pltpu.make_async_copy(weight.at[at], here.at[at], sems.at[h, i]) for i, at in enumerate(parts)])
        stores.append([pltpu.make_async_copy(logits.at[at], out.at[at], sems.at[h, 2 + i]) for i, at in enumerate(parts)])

    def start_placing(h):
        own, columns, _, _, hidden, _, _ = heads[h]
        placing.append(place(scalars, own, blocks, columns, hidden, half, place_sems.at[h]))

    def product(h, i):
        _, _, _, _, hidden, here, logits = heads[h]
        rows_product(here, hidden, logits, parts[i])
        stores[h][i].start()

    tiles = [slice(j * 128, (j + 1) * 128) for j in range(out_s.shape[1] // 128)]

    def put(j, row, value):
        side, k = divmod(j, 2)
        stats[:, side, pl.ds(row * 2 + k, 1), :] = jnp.broadcast_to(value[None], (stats.shape[0], 1, 128))

    loads[0][0].start()
    start_placing(0)
    wait_all(placing[0])
    loads[0][1].start()
    loads[0][0].wait()
    start_placing(1)
    product(0, 0)
    loads[0][1].wait()
    start_all(loads[1])
    product(0, 1)
    keep = pltpu.make_async_copy(hidden_s, out_hidden, sems.at[1, 4])
    keep.start()
    entry = lax.broadcasted_iota(I32, (out_s.shape[0], 128), 0) + scalars[15]
    for j, at in enumerate(tiles):
        s = logits_s[:, at]
        top = jnp.max(s, axis=0, keepdims=True)
        put(j, 0, top + jnp.log(jnp.sum(jnp.exp(s - top), axis=0, keepdims=True)))
        put(j, 3, jnp.sum(jnp.where(ids[:, at] == entry, s, 0.0), axis=0, keepdims=True))
    wait_all(placing[1])
    for i in range(2):
        loads[1][i].wait()
        product(1, i)
    for j, at in enumerate(tiles):
        t = logits_t[:, at]
        top = jnp.max(t, axis=0, keepdims=True)
        exp_t = jnp.exp(t - top)
        total = jnp.sum(exp_t, axis=0, keepdims=True)
        put(j, 1, top + jnp.log(total))
        put(j, 2, jnp.sum(exp_t * (t - logits_s[:, at]), axis=0, keepdims=True) / total)
    wait_all(stores[0])
    wait_all(stores[1])
    keep.wait()


def combine_kernel(every, out):
    stats = every[...]
    lse = stats[:, 0:4]
    top = jnp.max(lse, axis=0)
    total = top + jnp.log(jnp.sum(jnp.exp(lse - top[None]), axis=0))
    total_s, total_t = total[0:2], total[2:4]
    cross = jnp.sum(jnp.exp(stats[:, 2:4] - total_t[None]) * stats[:, 4:6], axis=0)
    picked = jnp.sum(stats[:, 6:8], axis=0)
    out[0:4] = total
    out[4:6] = cross - total_t + total_s
    out[6:8] = picked - total_s


def join_kernel(s_mine, t_mine, s_theirs, t_theirs, s_out, t_out, here, sems):
    rows = s_mine.shape[0]
    given = ((s_mine, t_mine), (s_theirs, t_theirs))
    loads = [
        pltpu.make_async_copy(given[side][h], here.at[h, pl.ds(side * rows, rows)], sems.at[2 * h + side])
        for h in range(2)
        for side in range(2)
    ]
    stores = [pltpu.make_async_copy(here.at[h], out, sems.at[4 + h]) for h, out in enumerate((s_out, t_out))]
    start_all(loads)
    for h in range(2):
        wait_all(loads[2 * h : 2 * h + 2])
        stores[h].start()
    wait_all(stores)


def share_kernel(
    scalars, mine, other, factor, student, teacher, weight_mine, weight_theirs, share, out_t,
    small, totals, s_here, t_here, grad, grad_t, weight, part, sems,
):
    rows, width = weight_theirs.shape
    tokens = student.shape[1]
    tile = weight.shape[2]
    steps = width // tile
    count = rows // 128
    figures = start_all(
        [pltpu.make_async_copy(mine, small.at[0], sems.at[4, 2]), pltpu.make_async_copy(other, small.at[1], sems.at[4, 3])]
    )
    logits = []
    for j in range(2 * count):
        at = pl.ds(j * 128, 128)
        logits.append(
            start_all(
                [
                    pltpu.make_async_copy(student.at[at], s_here.at[at], sems.at[0, j]),
                    pltpu.make_async_copy(teacher.at[at], t_here.at[at], sems.at[1, j]),
                ]
            )
        )
    waiting = []

    def load_weight():
        k = len(waiting)
        if k == steps:
            return
        columns = pl.ds(pl.multiple_of(scalars[0] * width + k * tile, 128), tile)
        waiting.append(
            start_all(
                [
                    pltpu.make_async_copy(weight_mine.at[:, columns], weight.at[k, pl.ds(0, rows)], sems.at[5, k]),
                    pltpu.make_async_copy(
                        weight_theirs.at[:, pl.ds(k * tile, tile)], weight.at[k, pl.ds(rows, rows)], sems.at[6, k]
                    ),
                ]
            )
        )

    load_weight()
    first = scalars[0] == 0
    wait_all(figures)
    low, high = jnp.where(first, small[0], small[1]), jnp.where(first, small[1], small[0])
    for j in range(tokens // 128):
        half, k = (low, high)[j // 2], j % 2
        for i in range(2):
            totals[i : i + 1, j * 128 : (j + 1) * 128] = half[2 * i + k : 2 * i + k + 1]
    stores = []
    for i, pair in enumerate(logits):
        wait_all(pair)
        at = slice(i * 128, (i + 1) * 128)
        value = factor[...] * (jnp.exp(s_here[at] - totals[0:1]) - jnp.exp(t_here[at] - totals[1:2]))
        if i < count:
            grad_t[at] = value.astype(BF16)
            stores.append(pltpu.make_async_copy(grad_t.at[pl.ds(i * 128, 128)], out_t.at[pl.ds(i * 128, 128)], sems.at[7, i]))
            stores[-1].start()
        grad[:, at] = value.T.astype(BF16)
        if i in (count - 1, 2 * count - 3):
            load_weight()
    written = 0
    for k in range(steps):
        wait_all(waiting[k])
        load_weight()
        product = jnp.dot(grad[...], weight[k], preferred_element_type=F32).astype(BF16)
        for j in range(tile // 256):
            high_at, low_at = divmod(k * tile + j * 256, share.shape[3])
            part[:, high_at, :, pl.ds(low_at, 256)] = product[:, j * 256 : (j + 1) * 256].reshape(share.shape[0], 16, 256)
        while (k + 1) * tile >= (written + 1) * share.shape[3]:
            stores.append(pltpu.make_async_copy(part.at[:, written], share.at[:, written], sems.at[4, written]))
            stores[-1].start()
            written += 1
    wait_all(stores)


def grad_weight_kernel(grad, hidden, out):
    out[...] = jnp.dot(grad[...], hidden[...], preferred_element_type=F32).astype(BF16)


def sum_kernel(parts, out):
    count = parts.shape[0] // 16
    total = jnp.sum(parts[0:count].astype(F32), axis=0)
    for i in range(1, 16):
        total += jnp.sum(parts[count * i : count * (i + 1)].astype(F32), axis=0)
    out[...] = jnp.broadcast_to(total.astype(BF16)[None], out.shape)


def assemble_kernel(scalars, mine, theirs, out):
    width = mine.shape[2]
    first = scalars[0] == 0
    low = jnp.where(first, mine[...], theirs[...])
    high = jnp.where(first, theirs[...], mine[...])
    for core, pieces in enumerate((low, high)):
        for v in range(8):
            column = (core * 2 + v % 2) * width
            out[v // 2 * 16 : v // 2 * 16 + 16, column : column + width] = pieces[v]


IN_VMEM = pl.BlockSpec(memory_space=pltpu.VMEM)
IN_HBM = pl.BlockSpec(memory_space=pltpu.HBM)
IN_SMEM = pl.BlockSpec(memory_space=pltpu.SMEM)


def params(limit=VMEM_BYTES):
    return pltpu.CompilerParams(vmem_limit_bytes=limit)


def shards(
    student_hidden,
    student_weight,
    teacher_hidden,
    teacher_weight,
    token_ids,
    group_ids,
    response_mask,
):
    own_rows = student_hidden.shape[0]
    half = own_rows // 2
    head_rows, width = student_weight.shape
    width_t = teacher_weight.shape[1]
    tokens = token_ids.shape[0]
    dp, vocab = lax.axis_index("dp"), lax.axis_index("vocab")
    core = vocab % 2
    odd = (vocab // 4) % 2
    half_width = width // 2
    scalars = jnp.stack(first_rows(core, odd, dp // 4, dp % 4, half) + [(dp * 16 + vocab) * head_rows]).astype(I32)
    core_scalar = core.astype(I32).reshape(1)

    kept = pl.pallas_call(
        half_kernel,
        in_specs=[IN_SMEM] + [IN_HBM] * 2,
        out_specs=IN_HBM,
        out_shape=jax.ShapeDtypeStruct((half, width + width_t), BF16),
        scratch_shapes=[pltpu.VMEM((half, width + width_t), BF16), pltpu.SemaphoreType.DMA((3,))],
        compiler_params=params(),
    )((core + odd - 2 * core * odd).astype(I32).reshape(1), student_hidden, teacher_hidden)
    same_group = group_ids[:, None] == group_ids[None, :]
    lengths = jnp.sum(same_group.astype(F32), axis=1)
    token_weight = (response_mask.astype(F32) * SPAN / lengths).reshape(1, tokens)
    weight_columns = lax.dynamic_slice_in_dim(student_weight, (1 - core) * half_width, half_width, 1)
    blocks, (scalars, core_scalar, token_weight, ids, weight_theirs) = gather_tokens(
        kept, (scalars, core_scalar, token_weight, token_ids.reshape(1, tokens), weight_columns)
    )

    student_logits, teacher_logits, stats, hidden = pl.pallas_call(
        functools.partial(logits_kernel, half),
        in_specs=[IN_SMEM] + [IN_VMEM] * 16 + [IN_HBM] * 2 + [IN_VMEM],
        out_specs=[IN_HBM] * 2 + [IN_VMEM, IN_HBM],
        out_shape=[
            jax.ShapeDtypeStruct((head_rows, tokens), F32),
            jax.ShapeDtypeStruct((head_rows, tokens), F32),
            jax.ShapeDtypeStruct((64, 2, 8, 128), F32),
            jax.ShapeDtypeStruct((tokens, width), BF16),
        ],
        scratch_shapes=[
            pltpu.VMEM((tokens, width), BF16),
            pltpu.VMEM((tokens, width_t), BF16),
            pltpu.VMEM((head_rows, width), BF16),
            pltpu.VMEM((head_rows, width_t), BF16),
            pltpu.VMEM((head_rows, tokens), F32),
            pltpu.VMEM((head_rows, tokens), F32),
            pltpu.SemaphoreType.DMA((2, 15)),
            pltpu.SemaphoreType.DMA((2, 5)),
        ],
        compiler_params=params(42 * 1024 * 1024),
        cost_estimate=pl.CostEstimate(
            flops=2 * head_rows * tokens * (width + width_t), bytes_accessed=24_000_000, transcendentals=2 * head_rows * tokens
        ),
    )(scalars, student_hidden, teacher_hidden, *blocks, student_weight, teacher_weight, ids)

    student_theirs, teacher_theirs = swap([student_logits, teacher_logits])
    every = lax.all_to_all(stats.reshape(128, 8, 128), BOTH, split_axis=0, concat_axis=0, tiled=True)
    both_s, both_t = pl.pallas_call(
        join_kernel,
        in_specs=[IN_HBM] * 4,
        out_specs=[IN_HBM] * 2,
        out_shape=[jax.ShapeDtypeStruct((2 * head_rows, tokens), F32)] * 2,
        scratch_shapes=[pltpu.VMEM((2, 2 * head_rows, tokens), F32), pltpu.SemaphoreType.DMA((6,))],
        compiler_params=params(),
        cost_estimate=pl.CostEstimate(flops=0, bytes_accessed=11_000_000, transcendentals=0),
    )(student_logits, teacher_logits, student_theirs, teacher_theirs)
    every, both_s, both_t = lax.optimization_barrier((every, both_s, both_t))
    mine = pl.pallas_call(
        combine_kernel,
        in_specs=[IN_VMEM],
        out_specs=IN_VMEM,
        out_shape=jax.ShapeDtypeStruct((8, 128), F32),
        compiler_params=params(4 * 1024 * 1024),
    )(every)
    other = send(mine, OTHER_CORE)

    groups, quarter = tokens // 16, half_width // 2
    share, grad_t = pl.pallas_call(
        share_kernel,
        in_specs=[IN_SMEM] + [IN_HBM] * 2 + [IN_VMEM] + [IN_HBM] * 4,
        out_specs=[IN_HBM, IN_HBM],
        out_shape=[
            jax.ShapeDtypeStruct((groups, 2, 16, quarter), BF16),
            jax.ShapeDtypeStruct((head_rows, tokens), BF16),
        ],
        scratch_shapes=[
            pltpu.VMEM((2, 8, 128), F32),
            pltpu.VMEM((8, tokens), F32),
            pltpu.VMEM((2 * head_rows, tokens), F32),
            pltpu.VMEM((2 * head_rows, tokens), F32),
            pltpu.VMEM((tokens, 2 * head_rows), BF16),
            pltpu.VMEM((head_rows, tokens), BF16),
            pltpu.VMEM((half_width // 512, 2 * head_rows, 512), BF16),
            pltpu.VMEM((groups, 2, 16, quarter), BF16),
            pltpu.SemaphoreType.DMA((8, 10)),
        ],
        compiler_params=params(),
        cost_estimate=pl.CostEstimate(flops=2 * head_rows * tokens * width, bytes_accessed=16_000_000, transcendentals=0),
    )(
        core_scalar, mine, other, token_weight, both_s, both_t, student_weight, weight_theirs,
    )
    parts = lax.all_to_all(
        share.reshape(64, 16, quarter), BOTH, split_axis=0, concat_axis=0, tiled=True, axis_index_groups=SAME_CORE
    )

    grad_weight = pl.pallas_call(
        grad_weight_kernel,
        grid=(width // 1024,),
        in_specs=[
            pl.BlockSpec((head_rows, tokens), lambda k: (0, 0)),
            pl.BlockSpec((tokens, 1024), lambda k: (0, k)),
        ],
        out_specs=pl.BlockSpec((head_rows, 1024), lambda k: (0, k)),
        out_shape=jax.ShapeDtypeStruct((head_rows, width), BF16),
        compiler_params=params(16 * 1024 * 1024),
        cost_estimate=pl.CostEstimate(flops=2 * head_rows * tokens * width, bytes_accessed=13_000_000, transcendentals=0),
    )(grad_t, hidden)
    low, high = jnp.where(core == 0, mine, other), jnp.where(core == 0, other, mine)
    kl_all = jnp.concatenate([low[4:6], high[4:6]]).reshape(tokens)
    logp_all = jnp.concatenate([low[6:8], high[6:8]]).reshape(tokens)
    kl_tok = lax.dynamic_slice_in_dim(kl_all, dp * own_rows, own_rows, 0)
    logp_tok = lax.dynamic_slice_in_dim(logp_all, dp * own_rows, own_rows, 0)
    parts, grad_weight, kl_tok, logp_tok = lax.optimization_barrier((parts, grad_weight, kl_tok, logp_tok))

    summed = pl.pallas_call(
        sum_kernel,
        in_specs=[IN_VMEM],
        out_specs=IN_VMEM,
        out_shape=jax.ShapeDtypeStruct((8, 16, quarter), BF16),
        compiler_params=params(8 * 1024 * 1024),
    )(parts)
    pieces_mine = lax.all_to_all(
        summed,
        BOTH, split_axis=0, concat_axis=0, tiled=True, axis_index_groups=SAME_TOKENS,
    )
    pieces_theirs = send(pieces_mine, OTHER_CORE)
    grad_hidden = pl.pallas_call(
        assemble_kernel,
        in_specs=[IN_SMEM] + [IN_VMEM] * 2,
        out_specs=IN_VMEM,
        out_shape=jax.ShapeDtypeStruct((own_rows, width), BF16),
        compiler_params=params(8 * 1024 * 1024),
    )(core_scalar, pieces_mine, pieces_theirs)
    return (kl_tok, logp_tok, grad_hidden, grad_weight)


def solution(mesh):
    in_specs = (
        P("dp", None),
        P(("dp", "vocab"), None),
        P("dp", None),
        P(("dp", "vocab"), None),
        P(),
        P(),
        P(),
    )
    out_specs = (P("dp"), P("dp"), P("dp", None), P(("dp", "vocab"), None))
    return jax.shard_map(shards, mesh=mesh, in_specs=in_specs, out_specs=out_specs, check_vma=False)
```

```python
import functools

import jax
import jax.numpy as jnp
from jax import lax
from jax.experimental import pallas as pl
from jax.experimental.pallas import tpu as pltpu
from jax.sharding import PartitionSpec as P

SPAN = 32
BOTH = ("dp", "vocab")
F32 = jnp.float32
BF16 = jnp.bfloat16
I32 = jnp.int32
VMEM_BYTES = 63 * 1024 * 1024


def coordinates(device):
    dp, vocab = divmod(device, 16)
    x_lo, z = divmod(dp, 4)
    y, rest = divmod(vocab, 4)
    x_hi, core = divmod(rest, 2)
    return x_hi * 2 + x_lo, y, z, core


def device_at(x, y, z, core):
    x_hi, x_lo = divmod(x % 4, 2)
    return (x_lo * 4 + z % 4) * 16 + (y % 4) * 4 + x_hi * 2 + core


def permutation(move):
    return [(i, device_at(*move(*coordinates(i)))) for i in range(128)]


def way(core):
    return 1 - 2 * core


ALONG_Z = permutation(lambda x, y, z, c: (x, y, z + way(c), c))
ALONG_X = permutation(lambda x, y, z, c: (x + way(c), y, z, c))
ALONG_Y = permutation(lambda x, y, z, c: (x, y + way(c), z, c))
OTHER_CORE = permutation(lambda x, y, z, c: (x, y, z, 1 - c))
SAME_TOKENS = [[dp * 16 + v * 2 + c for v in range(8)] for dp in range(8) for c in range(2)]
SAME_CORE = [[i for i in range(128) if i % 2 == c] for c in range(2)]


def send(value, where):
    return lax.ppermute(value, BOTH, where)


def after(done, then):
    both = lax.optimization_barrier((done, then))
    return both


def swap(blocks):
    return [send(block, OTHER_CORE) for block in blocks]


def gather_tokens(kept, others):
    near_z, near_x, others = lax.optimization_barrier((send(kept, ALONG_Z), send(kept, ALONG_X), others))
    second = [send(near_z, ALONG_X), send(near_z, ALONG_Z), send(near_z, ALONG_Y)] + swap([near_z, near_x])
    near_zx, far_z, rest_z, o_near_z, o_near_x = lax.optimization_barrier(second)
    far_zx, rest_zx = send(far_z, ALONG_X), send(near_zx, ALONG_Y)
    far_zx, o_near_zx, o_far_z, rest_z = lax.optimization_barrier((far_zx, *swap([near_zx, far_z]), rest_z))
    o_rest_z, o_far_zx, o_rest_zx = swap([rest_z, far_zx, rest_zx])
    scalars, core_scalar, token_weight, ids, weight_columns = others
    o_rest_z, o_far_zx, o_rest_zx, weight_columns = lax.optimization_barrier((o_rest_z, o_far_zx, o_rest_zx, weight_columns))
    weight_theirs = send(weight_columns, OTHER_CORE)
    mine = [near_z, rest_z, near_x, far_z, near_zx, rest_zx, far_zx]
    theirs = [o_near_z, o_rest_z, o_near_x, o_far_z, o_near_zx, o_rest_zx, o_far_zx]
    return mine + theirs, (scalars, core_scalar, token_weight, ids, weight_theirs)


def first_rows(core, odd, x_lo, z, half):
    def block(xl, zz):
        return (xl * 4 + jnp.remainder(zz, 4)) * 2

    def arrived(c):
        s = 1 - 2 * c
        k = c + odd - 2 * c * odd
        return [
            block(x_lo, z - s) + k,
            block(x_lo, z - s) + 1 - k,
            block(1 - x_lo, z) + k,
            block(x_lo, z + 2) + k,
            block(1 - x_lo, z - s) + k,
            block(1 - x_lo, z - s) + 1 - k,
            block(1 - x_lo, z + 2) + k,
        ]

    return [half * b for b in [block(x_lo, z)] + arrived(core) + arrived(1 - core)]


def start_all(copies):
    for copy in copies:
        copy.start()
    return copies


def wait_all(copies):
    for copy in copies:
        copy.wait()


def half_kernel(scalars, student, teacher, out, here, sems):
    half, width = out.shape[0], student.shape[1]
    rows = pl.ds(pl.multiple_of(scalars[0] * half, half), half)
    loads = [
        pltpu.make_async_copy(student.at[rows], here.at[:, pl.ds(0, width)], sems.at[0]),
        pltpu.make_async_copy(teacher.at[rows], here.at[:, pl.ds(width, teacher.shape[1])], sems.at[1]),
    ]
    wait_all(start_all(loads))
    store = pltpu.make_async_copy(here, out, sems.at[2])
    store.start()
    store.wait()


def place(scalars, own, blocks, columns, hidden, half, sems):
    copies = []
    for i, block in enumerate([own] + [b.at[:, columns] for b in blocks]):
        rows = pl.ds(pl.multiple_of(scalars[i], half), own.shape[0] if i == 0 else half)
        copies.append(pltpu.make_async_copy(block, hidden.at[rows], sems.at[i]))
    return start_all(copies)


def rows_product(weight, hidden, out, at):
    out[at] = lax.dot_general(weight[at], hidden[...], (((1,), (1,)), ((), ())), preferred_element_type=F32)


def logits_kernel(half, scalars, own_s, own_t, *refs):
    blocks = refs[:14]
    weight_s, weight_t, ids, out_s, out_t, stats, out_hidden = refs[14:21]
    hidden_s, hidden_t, here_s, here_t, logits_s, logits_t, place_sems, sems = refs[21:]
    rows = out_s.shape[0] // 2
    width_s, width_t = hidden_s.shape[1], hidden_t.shape[1]
    parts = [slice(i * rows, (i + 1) * rows) for i in range(2)]
    heads = [
        (own_s, pl.ds(0, width_s), weight_s, out_s, hidden_s, here_s, logits_s),
        (own_t, pl.ds(width_s, width_t), weight_t, out_t, hidden_t, here_t, logits_t),
    ]
    placing, loads, stores = [], [], []
    for h, (own, columns, weight, out, hidden, here, logits) in enumerate(heads):
        loads.append([pltpu.make_async_copy(weight.at[at], here.at[at], sems.at[h, i]) for i, at in enumerate(parts)])
        stores.append([pltpu.make_async_copy(logits.at[at], out.at[at], sems.at[h, 2 + i]) for i, at in enumerate(parts)])

    def start_placing(h):
        own, columns, _, _, hidden, _, _ = heads[h]
        placing.append(place(scalars, own, blocks, columns, hidden, half, place_sems.at[h]))

    def product(h, i):
        _, _, _, _, hidden, here, logits = heads[h]
        rows_product(here, hidden, logits, parts[i])
        stores[h][i].start()

    tiles = [slice(j * 128, (j + 1) * 128) for j in range(out_s.shape[1] // 128)]

    def put(j, row, value):
        side, k = divmod(j, 2)
        stats[:, side, pl.ds(row * 2 + k, 1), :] = jnp.broadcast_to(value[None], (stats.shape[0], 1, 128))

    loads[0][0].start()
    start_placing(0)
    wait_all(placing[0])
    loads[0][1].start()
    loads[0][0].wait()
    start_placing(1)
    product(0, 0)
    loads[0][1].wait()
    start_all(loads[1])
    product(0, 1)
    keep = pltpu.make_async_copy(hidden_s, out_hidden, sems.at[1, 4])
    keep.start()
    entry = lax.broadcasted_iota(I32, (out_s.shape[0], 128), 0) + scalars[15]
    for j, at in enumerate(tiles):
        s = logits_s[:, at]
        top = jnp.max(s, axis=0, keepdims=True)
        put(j, 0, top + jnp.log(jnp.sum(jnp.exp(s - top), axis=0, keepdims=True)))
        put(j, 3, jnp.sum(jnp.where(ids[:, at] == entry, s, 0.0), axis=0, keepdims=True))
    wait_all(placing[1])
    for i in range(2):
        loads[1][i].wait()
        product(1, i)
    for j, at in enumerate(tiles):
        t = logits_t[:, at]
        top = jnp.max(t, axis=0, keepdims=True)
        exp_t = jnp.exp(t - top)
        total = jnp.sum(exp_t, axis=0, keepdims=True)
        put(j, 1, top + jnp.log(total))
        put(j, 2, jnp.sum(exp_t * (t - logits_s[:, at]), axis=0, keepdims=True) / total)
    wait_all(stores[0])
    wait_all(stores[1])
    keep.wait()


def combine_kernel(every, out):
    stats = every[...]
    lse = stats[:, 0:4]
    top = jnp.max(lse, axis=0)
    total = top + jnp.log(jnp.sum(jnp.exp(lse - top[None]), axis=0))
    total_s, total_t = total[0:2], total[2:4]
    cross = jnp.sum(jnp.exp(stats[:, 2:4] - total_t[None]) * stats[:, 4:6], axis=0)
    picked = jnp.sum(stats[:, 6:8], axis=0)
    out[0:4] = total
    out[4:6] = cross - total_t + total_s
    out[6:8] = picked - total_s


def join_kernel(s_mine, t_mine, s_theirs, t_theirs, s_out, t_out, here, sems):
    rows = s_mine.shape[0]
    given = ((s_mine, t_mine), (s_theirs, t_theirs))
    loads = [
        pltpu.make_async_copy(given[side][h], here.at[h, pl.ds(side * rows, rows)], sems.at[2 * h + side])
        for h in range(2)
        for side in range(2)
    ]
    stores = [pltpu.make_async_copy(here.at[h], out, sems.at[4 + h]) for h, out in enumerate((s_out, t_out))]
    start_all(loads)
    for h in range(2):
        wait_all(loads[2 * h : 2 * h + 2])
        stores[h].start()
    wait_all(stores)


def share_kernel(
    scalars, mine, other, factor, student, teacher, weight_mine, weight_theirs, share, out_t,
    small, totals, s_here, t_here, grad, grad_t, weight, part, sems,
):
    rows, width = weight_theirs.shape
    tokens = student.shape[1]
    tile = weight.shape[2]
    steps = width // tile
    count = rows // 128
    figures = start_all(
        [pltpu.make_async_copy(mine, small.at[0], sems.at[4, 2]), pltpu.make_async_copy(other, small.at[1], sems.at[4, 3])]
    )
    logits = []
    for j in range(2 * count):
        at = pl.ds(j * 128, 128)
        logits.append(
            start_all(
                [
                    pltpu.make_async_copy(student.at[at], s_here.at[at], sems.at[0, j]),
                    pltpu.make_async_copy(teacher.at[at], t_here.at[at], sems.at[1, j]),
                ]
            )
        )
    waiting = []

    def load_weight():
        k = len(waiting)
        if k == steps:
            return
        columns = pl.ds(pl.multiple_of(scalars[0] * width + k * tile, 128), tile)
        waiting.append(
            start_all(
                [
                    pltpu.make_async_copy(weight_mine.at[:, columns], weight.at[k, pl.ds(0, rows)], sems.at[5, k]),
                    pltpu.make_async_copy(
                        weight_theirs.at[:, pl.ds(k * tile, tile)], weight.at[k, pl.ds(rows, rows)], sems.at[6, k]
                    ),
                ]
            )
        )

    load_weight()
    first = scalars[0] == 0
    wait_all(figures)
    low, high = jnp.where(first, small[0], small[1]), jnp.where(first, small[1], small[0])
    for j in range(tokens // 128):
        half, k = (low, high)[j // 2], j % 2
        for i in range(2):
            totals[i : i + 1, j * 128 : (j + 1) * 128] = half[2 * i + k : 2 * i + k + 1]
    stores = []
    for i, pair in enumerate(logits):
        wait_all(pair)
        at = slice(i * 128, (i + 1) * 128)
        value = factor[...] * (jnp.exp(s_here[at] - totals[0:1]) - jnp.exp(t_here[at] - totals[1:2]))
        if i < count:
            grad_t[at] = value.astype(BF16)
            stores.append(pltpu.make_async_copy(grad_t.at[pl.ds(i * 128, 128)], out_t.at[pl.ds(i * 128, 128)], sems.at[7, i]))
            stores[-1].start()
        grad[:, at] = value.T.astype(BF16)
        if i in (count - 1, 2 * count - 3):
            load_weight()
    written = 0
    for k in range(steps):
        wait_all(waiting[k])
        load_weight()
        product = jnp.dot(grad[...], weight[k], preferred_element_type=F32).astype(BF16)
        for j in range(tile // 256):
            high_at, low_at = divmod(k * tile + j * 256, share.shape[3])
            part[:, high_at, :, pl.ds(low_at, 256)] = product[:, j * 256 : (j + 1) * 256].reshape(share.shape[0], 16, 256)
        while (k + 1) * tile >= (written + 1) * share.shape[3]:
            stores.append(pltpu.make_async_copy(part.at[:, written], share.at[:, written], sems.at[4, written]))
            stores[-1].start()
            written += 1
    wait_all(stores)


def grad_weight_kernel(grad, hidden, out):
    out[...] = jnp.dot(grad[...], hidden[...], preferred_element_type=F32).astype(BF16)


def sum_kernel(parts, out):
    count = parts.shape[0] // 16
    total = jnp.sum(parts[0:count].astype(F32), axis=0)
    for i in range(1, 16):
        total += jnp.sum(parts[count * i : count * (i + 1)].astype(F32), axis=0)
    out[...] = jnp.broadcast_to(total.astype(BF16)[None], out.shape)


def assemble_kernel(scalars, mine, theirs, out):
    width = mine.shape[2]
    first = scalars[0] == 0
    low = jnp.where(first, mine[...], theirs[...])
    high = jnp.where(first, theirs[...], mine[...])
    for core, pieces in enumerate((low, high)):
        for v in range(8):
            column = (core * 2 + v % 2) * width
            out[v // 2 * 16 : v // 2 * 16 + 16, column : column + width] = pieces[v]


IN_VMEM = pl.BlockSpec(memory_space=pltpu.VMEM)
IN_HBM = pl.BlockSpec(memory_space=pltpu.HBM)
IN_SMEM = pl.BlockSpec(memory_space=pltpu.SMEM)


def params(limit=VMEM_BYTES):
    return pltpu.CompilerParams(vmem_limit_bytes=limit)


def shards(
    student_hidden,
    student_weight,
    teacher_hidden,
    teacher_weight,
    token_ids,
    group_ids,
    response_mask,
):
    own_rows = student_hidden.shape[0]
    half = own_rows // 2
    head_rows, width = student_weight.shape
    width_t = teacher_weight.shape[1]
    tokens = token_ids.shape[0]
    dp, vocab = lax.axis_index("dp"), lax.axis_index("vocab")
    core = vocab % 2
    odd = (vocab // 4) % 2
    half_width = width // 2
    scalars = jnp.stack(first_rows(core, odd, dp // 4, dp % 4, half) + [(dp * 16 + vocab) * head_rows]).astype(I32)
    core_scalar = core.astype(I32).reshape(1)

    kept = pl.pallas_call(
        half_kernel,
        in_specs=[IN_SMEM] + [IN_HBM] * 2,
        out_specs=IN_HBM,
        out_shape=jax.ShapeDtypeStruct((half, width + width_t), BF16),
        scratch_shapes=[pltpu.VMEM((half, width + width_t), BF16), pltpu.SemaphoreType.DMA((3,))],
        compiler_params=params(),
    )((core + odd - 2 * core * odd).astype(I32).reshape(1), student_hidden, teacher_hidden)
    same_group = group_ids[:, None] == group_ids[None, :]
    lengths = jnp.sum(same_group.astype(F32), axis=1)
    token_weight = (response_mask.astype(F32) * SPAN / lengths).reshape(1, tokens)
    weight_columns = lax.dynamic_slice_in_dim(student_weight, (1 - core) * half_width, half_width, 1)
    blocks, (scalars, core_scalar, token_weight, ids, weight_theirs) = gather_tokens(
        kept, (scalars, core_scalar, token_weight, token_ids.reshape(1, tokens), weight_columns)
    )

    student_logits, teacher_logits, stats, hidden = pl.pallas_call(
        functools.partial(logits_kernel, half),
        in_specs=[IN_SMEM] + [IN_VMEM] * 16 + [IN_HBM] * 2 + [IN_VMEM],
        out_specs=[IN_HBM] * 2 + [IN_VMEM, IN_HBM],
        out_shape=[
            jax.ShapeDtypeStruct((head_rows, tokens), F32),
            jax.ShapeDtypeStruct((head_rows, tokens), F32),
            jax.ShapeDtypeStruct((64, 2, 8, 128), F32),
            jax.ShapeDtypeStruct((tokens, width), BF16),
        ],
        scratch_shapes=[
            pltpu.VMEM((tokens, width), BF16),
            pltpu.VMEM((tokens, width_t), BF16),
            pltpu.VMEM((head_rows, width), BF16),
            pltpu.VMEM((head_rows, width_t), BF16),
            pltpu.VMEM((head_rows, tokens), F32),
            pltpu.VMEM((head_rows, tokens), F32),
            pltpu.SemaphoreType.DMA((2, 15)),
            pltpu.SemaphoreType.DMA((2, 5)),
        ],
        compiler_params=params(42 * 1024 * 1024),
        cost_estimate=pl.CostEstimate(
            flops=2 * head_rows * tokens * (width + width_t), bytes_accessed=24_000_000, transcendentals=2 * head_rows * tokens
        ),
    )(scalars, student_hidden, teacher_hidden, *blocks, student_weight, teacher_weight, ids)

    student_theirs, teacher_theirs = swap([student_logits, teacher_logits])
    every = lax.all_to_all(stats.reshape(128, 8, 128), BOTH, split_axis=0, concat_axis=0, tiled=True)
    both_s, both_t = pl.pallas_call(
        join_kernel,
        in_specs=[IN_HBM] * 4,
        out_specs=[IN_HBM] * 2,
        out_shape=[jax.ShapeDtypeStruct((2 * head_rows, tokens), F32)] * 2,
        scratch_shapes=[pltpu.VMEM((2, 2 * head_rows, tokens), F32), pltpu.SemaphoreType.DMA((6,))],
        compiler_params=params(),
        cost_estimate=pl.CostEstimate(flops=0, bytes_accessed=11_000_000, transcendentals=0),
    )(student_logits, teacher_logits, student_theirs, teacher_theirs)
    every, both_s, both_t = lax.optimization_barrier((every, both_s, both_t))
    mine = pl.pallas_call(
        combine_kernel,
        in_specs=[IN_VMEM],
        out_specs=IN_VMEM,
        out_shape=jax.ShapeDtypeStruct((8, 128), F32),
        compiler_params=params(4 * 1024 * 1024),
    )(every)
    other = send(mine, OTHER_CORE)

    groups, quarter = tokens // 16, half_width // 2
    share, grad_t = pl.pallas_call(
        share_kernel,
        in_specs=[IN_SMEM] + [IN_HBM] * 2 + [IN_VMEM] + [IN_HBM] * 4,
        out_specs=[IN_HBM, IN_HBM],
        out_shape=[
            jax.ShapeDtypeStruct((groups, 2, 16, quarter), BF16),
            jax.ShapeDtypeStruct((head_rows, tokens), BF16),
        ],
        scratch_shapes=[
            pltpu.VMEM((2, 8, 128), F32),
            pltpu.VMEM((8, tokens), F32),
            pltpu.VMEM((2 * head_rows, tokens), F32),
            pltpu.VMEM((2 * head_rows, tokens), F32),
            pltpu.VMEM((tokens, 2 * head_rows), BF16),
            pltpu.VMEM((head_rows, tokens), BF16),
            pltpu.VMEM((half_width // 512, 2 * head_rows, 512), BF16),
            pltpu.VMEM((groups, 2, 16, quarter), BF16),
            pltpu.SemaphoreType.DMA((8, 10)),
        ],
        compiler_params=params(),
        cost_estimate=pl.CostEstimate(flops=2 * head_rows * tokens * width, bytes_accessed=16_000_000, transcendentals=0),
    )(
        core_scalar, mine, other, token_weight, both_s, both_t, student_weight, weight_theirs,
    )
    parts = lax.all_to_all(
        share.reshape(64, 16, quarter), BOTH, split_axis=0, concat_axis=0, tiled=True, axis_index_groups=SAME_CORE
    )

    grad_weight = pl.pallas_call(
        grad_weight_kernel,
        grid=(width // 1024,),
        in_specs=[
            pl.BlockSpec((head_rows, tokens), lambda k: (0, 0)),
            pl.BlockSpec((tokens, 1024), lambda k: (0, k)),
        ],
        out_specs=pl.BlockSpec((head_rows, 1024), lambda k: (0, k)),
        out_shape=jax.ShapeDtypeStruct((head_rows, width), BF16),
        compiler_params=params(16 * 1024 * 1024),
        cost_estimate=pl.CostEstimate(flops=2 * head_rows * tokens * width, bytes_accessed=13_000_000, transcendentals=0),
    )(grad_t, hidden)
    low, high = jnp.where(core == 0, mine, other), jnp.where(core == 0, other, mine)
    kl_all = jnp.concatenate([low[4:6], high[4:6]]).reshape(tokens)
    logp_all = jnp.concatenate([low[6:8], high[6:8]]).reshape(tokens)
    kl_tok = lax.dynamic_slice_in_dim(kl_all, dp * own_rows, own_rows, 0)
    logp_tok = lax.dynamic_slice_in_dim(logp_all, dp * own_rows, own_rows, 0)
    parts, grad_weight, kl_tok, logp_tok = lax.optimization_barrier((parts, grad_weight, kl_tok, logp_tok))

    summed = pl.pallas_call(
        sum_kernel,
        in_specs=[IN_VMEM],
        out_specs=IN_VMEM,
        out_shape=jax.ShapeDtypeStruct((8, 16, quarter), BF16),
        compiler_params=params(8 * 1024 * 1024),
    )(parts)
    pieces_mine = lax.all_to_all(
        summed,
        BOTH, split_axis=0, concat_axis=0, tiled=True, axis_index_groups=SAME_TOKENS,
    )
    pieces_theirs = send(pieces_mine, OTHER_CORE)
    grad_hidden = pl.pallas_call(
        assemble_kernel,
        in_specs=[IN_SMEM] + [IN_VMEM] * 2,
        out_specs=IN_VMEM,
        out_shape=jax.ShapeDtypeStruct((own_rows, width), BF16),
        compiler_params=params(8 * 1024 * 1024),
    )(core_scalar, pieces_mine, pieces_theirs)
    return (kl_tok, logp_tok, grad_hidden, grad_weight)


def solution(mesh):
    in_specs = (
        P("dp", None),
        P(("dp", "vocab"), None),
        P("dp", None),
        P(("dp", "vocab"), None),
        P(),
        P(),
        P(),
    )
    out_specs = (P("dp"), P("dp"), P("dp", None), P(("dp", "vocab"), None))
    return jax.shard_map(shards, mesh=mesh, in_specs=in_specs, out_specs=out_specs, check_vma=False)
```

```python
import functools

import jax
import jax.numpy as jnp
from jax import lax
from jax.experimental import pallas as pl
from jax.experimental.pallas import tpu as pltpu
from jax.sharding import PartitionSpec as P

SPAN = 32
BOTH = ("dp", "vocab")
F32 = jnp.float32
BF16 = jnp.bfloat16
I32 = jnp.int32
VMEM_BYTES = 63 * 1024 * 1024


def coordinates(device):
    dp, vocab = divmod(device, 16)
    x_lo, z = divmod(dp, 4)
    y, rest = divmod(vocab, 4)
    x_hi, core = divmod(rest, 2)
    return x_hi * 2 + x_lo, y, z, core


def device_at(x, y, z, core):
    x_hi, x_lo = divmod(x % 4, 2)
    return (x_lo * 4 + z % 4) * 16 + (y % 4) * 4 + x_hi * 2 + core


def permutation(move):
    return [(i, device_at(*move(*coordinates(i)))) for i in range(128)]


def way(core):
    return 1 - 2 * core


ALONG_Z = permutation(lambda x, y, z, c: (x, y, z + way(c), c))
ALONG_X = permutation(lambda x, y, z, c: (x + way(c), y, z, c))
ALONG_Y = permutation(lambda x, y, z, c: (x, y + way(c), z, c))
OTHER_CORE = permutation(lambda x, y, z, c: (x, y, z, 1 - c))
SAME_TOKENS = [[dp * 16 + v * 2 + c for v in range(8)] for dp in range(8) for c in range(2)]
SAME_CORE = [[i for i in range(128) if i % 2 == c] for c in range(2)]


def send(value, where):
    return lax.ppermute(value, BOTH, where)


def after(done, then):
    both = lax.optimization_barrier((done, then))
    return both


def swap(blocks):
    return [send(block, OTHER_CORE) for block in blocks]


def gather_tokens(kept, others):
    near_z, near_x, others = lax.optimization_barrier((send(kept, ALONG_Z), send(kept, ALONG_X), others))
    second = [send(near_z, ALONG_X), send(near_z, ALONG_Z), send(near_z, ALONG_Y)] + swap([near_z, near_x])
    near_zx, far_z, rest_z, o_near_z, o_near_x = lax.optimization_barrier(second)
    far_zx, rest_zx = send(far_z, ALONG_X), send(near_zx, ALONG_Y)
    far_zx, o_near_zx, o_far_z, rest_z = lax.optimization_barrier((far_zx, *swap([near_zx, far_z]), rest_z))
    o_rest_z, o_far_zx, o_rest_zx = swap([rest_z, far_zx, rest_zx])
    scalars, core_scalar, token_weight, ids, weight_columns = others
    mine = [near_z, rest_z, near_x, far_z, near_zx, rest_zx, far_zx]
    theirs = [o_near_z, o_rest_z, o_near_x, o_far_z, o_near_zx, o_rest_zx, o_far_zx]
    return mine + theirs, (scalars, core_scalar, token_weight, ids, weight_columns)


def first_rows(core, odd, x_lo, z, half):
    def block(xl, zz):
        return (xl * 4 + jnp.remainder(zz, 4)) * 2

    def arrived(c):
        s = 1 - 2 * c
        k = c + odd - 2 * c * odd
        return [
            block(x_lo, z - s) + k,
            block(x_lo, z - s) + 1 - k,
            block(1 - x_lo, z) + k,
            block(x_lo, z + 2) + k,
            block(1 - x_lo, z - s) + k,
            block(1 - x_lo, z - s) + 1 - k,
            block(1 - x_lo, z + 2) + k,
        ]

    return [half * b for b in [block(x_lo, z)] + arrived(core) + arrived(1 - core)]


def start_all(copies):
    for copy in copies:
        copy.start()
    return copies


def wait_all(copies):
    for copy in copies:
        copy.wait()


def half_kernel(scalars, student, teacher, out, here, sems):
    half, width = out.shape[0], student.shape[1]
    rows = pl.ds(pl.multiple_of(scalars[0] * half, half), half)
    loads = [
        pltpu.make_async_copy(student.at[rows], here.at[:, pl.ds(0, width)], sems.at[0]),
        pltpu.make_async_copy(teacher.at[rows], here.at[:, pl.ds(width, teacher.shape[1])], sems.at[1]),
    ]
    wait_all(start_all(loads))
    store = pltpu.make_async_copy(here, out, sems.at[2])
    store.start()
    store.wait()


def place(scalars, own, blocks, columns, hidden, half, sems):
    copies = []
    for i, block in enumerate([own] + [b.at[:, columns] for b in blocks]):
        rows = pl.ds(pl.multiple_of(scalars[i], half), own.shape[0] if i == 0 else half)
        copies.append(pltpu.make_async_copy(block, hidden.at[rows], sems.at[i]))
    return start_all(copies)


def rows_product(weight, hidden, out, at):
    out[at] = lax.dot_general(weight[at], hidden[...], (((1,), (1,)), ((), ())), preferred_element_type=F32)


def logits_kernel(half, scalars, own_s, own_t, *refs):
    blocks = refs[:14]
    weight_s, weight_t, ids, out_s, out_t, stats, out_hidden = refs[14:21]
    hidden_s, hidden_t, here_s, here_t, logits_s, logits_t, place_sems, sems = refs[21:]
    rows = out_s.shape[0] // 2
    width_s, width_t = hidden_s.shape[1], hidden_t.shape[1]
    parts = [slice(i * rows, (i + 1) * rows) for i in range(2)]
    heads = [
        (own_s, pl.ds(0, width_s), weight_s, out_s, hidden_s, here_s, logits_s),
        (own_t, pl.ds(width_s, width_t), weight_t, out_t, hidden_t, here_t, logits_t),
    ]
    placing, loads, stores = [], [], []
    for h, (own, columns, weight, out, hidden, here, logits) in enumerate(heads):
        loads.append([pltpu.make_async_copy(weight.at[at], here.at[at], sems.at[h, i]) for i, at in enumerate(parts)])
        stores.append([pltpu.make_async_copy(logits.at[at], out.at[at], sems.at[h, 2 + i]) for i, at in enumerate(parts)])

    def start_placing(h):
        own, columns, _, _, hidden, _, _ = heads[h]
        placing.append(place(scalars, own, blocks, columns, hidden, half, place_sems.at[h]))

    def product(h, i):
        _, _, _, _, hidden, here, logits = heads[h]
        rows_product(here, hidden, logits, parts[i])
        stores[h][i].start()

    tiles = [slice(j * 128, (j + 1) * 128) for j in range(out_s.shape[1] // 128)]

    def put(j, row, value):
        side, k = divmod(j, 2)
        stats[:, side, pl.ds(row * 2 + k, 1), :] = jnp.broadcast_to(value[None], (stats.shape[0], 1, 128))

    loads[0][0].start()
    start_placing(0)
    wait_all(placing[0])
    loads[0][1].start()
    loads[0][0].wait()
    start_placing(1)
    product(0, 0)
    loads[0][1].wait()
    start_all(loads[1])
    product(0, 1)
    keep = pltpu.make_async_copy(hidden_s, out_hidden, sems.at[1, 4])
    keep.start()
    entry = lax.broadcasted_iota(I32, (out_s.shape[0], 128), 0) + scalars[15]
    for j, at in enumerate(tiles):
        s = logits_s[:, at]
        top = jnp.max(s, axis=0, keepdims=True)
        put(j, 0, top + jnp.log(jnp.sum(jnp.exp(s - top), axis=0, keepdims=True)))
        put(j, 3, jnp.sum(jnp.where(ids[:, at] == entry, s, 0.0), axis=0, keepdims=True))
    wait_all(placing[1])
    for i in range(2):
        loads[1][i].wait()
        product(1, i)
    for j, at in enumerate(tiles):
        t = logits_t[:, at]
        top = jnp.max(t, axis=0, keepdims=True)
        exp_t = jnp.exp(t - top)
        total = jnp.sum(exp_t, axis=0, keepdims=True)
        put(j, 1, top + jnp.log(total))
        put(j, 2, jnp.sum(exp_t * (t - logits_s[:, at]), axis=0, keepdims=True) / total)
    wait_all(stores[0])
    wait_all(stores[1])
    keep.wait()


def combine_kernel(every, out):
    stats = every[...]
    lse = stats[:, 0:4]
    top = jnp.max(lse, axis=0)
    total = top + jnp.log(jnp.sum(jnp.exp(lse - top[None]), axis=0))
    total_s, total_t = total[0:2], total[2:4]
    cross = jnp.sum(jnp.exp(stats[:, 2:4] - total_t[None]) * stats[:, 4:6], axis=0)
    picked = jnp.sum(stats[:, 6:8], axis=0)
    out[0:4] = total
    out[4:6] = cross - total_t + total_s
    out[6:8] = picked - total_s


def join_kernel(s_mine, t_mine, s_theirs, t_theirs, s_out, t_out, here, sems):
    rows = s_mine.shape[0]
    given = ((s_mine, t_mine), (s_theirs, t_theirs))
    loads = [
        pltpu.make_async_copy(given[side][h], here.at[h, pl.ds(side * rows, rows)], sems.at[2 * h + side])
        for h in range(2)
        for side in range(2)
    ]
    stores = [pltpu.make_async_copy(here.at[h], out, sems.at[4 + h]) for h, out in enumerate((s_out, t_out))]
    start_all(loads)
    for h in range(2):
        wait_all(loads[2 * h : 2 * h + 2])
        stores[h].start()
    wait_all(stores)


def share_kernel(
    scalars, mine, other, factor, student, teacher, weight_mine, weight_theirs, share, out_t,
    small, totals, s_here, t_here, grad, grad_t, weight, part, sems,
):
    rows, width = weight_theirs.shape
    tokens = student.shape[1]
    tile = weight.shape[2]
    steps = width // tile
    count = rows // 128
    figures = start_all(
        [pltpu.make_async_copy(mine, small.at[0], sems.at[4, 2]), pltpu.make_async_copy(other, small.at[1], sems.at[4, 3])]
    )
    logits = []
    for j in range(2 * count):
        at = pl.ds(j * 128, 128)
        logits.append(
            start_all(
                [
                    pltpu.make_async_copy(student.at[at], s_here.at[at], sems.at[0, j]),
                    pltpu.make_async_copy(teacher.at[at], t_here.at[at], sems.at[1, j]),
                ]
            )
        )
    waiting = []

    def load_weight():
        k = len(waiting)
        if k == steps:
            return
        columns = pl.ds(pl.multiple_of(scalars[0] * width + k * tile, 128), tile)
        waiting.append(
            start_all(
                [
                    pltpu.make_async_copy(weight_mine.at[:, columns], weight.at[k, pl.ds(0, rows)], sems.at[5, k]),
                    pltpu.make_async_copy(
                        weight_theirs.at[:, pl.ds(k * tile, tile)], weight.at[k, pl.ds(rows, rows)], sems.at[6, k]
                    ),
                ]
            )
        )

    load_weight()
    first = scalars[0] == 0
    wait_all(figures)
    low, high = jnp.where(first, small[0], small[1]), jnp.where(first, small[1], small[0])
    for j in range(tokens // 128):
        half, k = (low, high)[j // 2], j % 2
        for i in range(2):
            totals[i : i + 1, j * 128 : (j + 1) * 128] = half[2 * i + k : 2 * i + k + 1]
    stores = []
    for i, pair in enumerate(logits):
        wait_all(pair)
        at = slice(i * 128, (i + 1) * 128)
        value = factor[...] * (jnp.exp(s_here[at] - totals[0:1]) - jnp.exp(t_here[at] - totals[1:2]))
        if i < count:
            grad_t[at] = value.astype(BF16)
            stores.append(pltpu.make_async_copy(grad_t.at[pl.ds(i * 128, 128)], out_t.at[pl.ds(i * 128, 128)], sems.at[7, i]))
            stores[-1].start()
        grad[:, at] = value.T.astype(BF16)
        if i in (count - 1, 2 * count - 3):
            load_weight()
    written = 0
    for k in range(steps):
        wait_all(waiting[k])
        load_weight()
        product = jnp.dot(grad[...], weight[k], preferred_element_type=F32).astype(BF16)
        for j in range(tile // 256):
            high_at, low_at = divmod(k * tile + j * 256, share.shape[3])
            part[:, high_at, :, pl.ds(low_at, 256)] = product[:, j * 256 : (j + 1) * 256].reshape(share.shape[0], 16, 256)
        while (k + 1) * tile >= (written + 1) * share.shape[3]:
            stores.append(pltpu.make_async_copy(part.at[:, written], share.at[:, written], sems.at[4, written]))
            stores[-1].start()
            written += 1
    wait_all(stores)


def grad_weight_kernel(grad, hidden, out):
    out[...] = jnp.dot(grad[...], hidden[...], preferred_element_type=F32).astype(BF16)


def sum_kernel(parts, out):
    count = parts.shape[0] // 16
    total = jnp.sum(parts[0:count].astype(F32), axis=0)
    for i in range(1, 16):
        total += jnp.sum(parts[count * i : count * (i + 1)].astype(F32), axis=0)
    out[...] = jnp.broadcast_to(total.astype(BF16)[None], out.shape)


def assemble_kernel(scalars, mine, theirs, out):
    width = mine.shape[2]
    first = scalars[0] == 0
    low = jnp.where(first, mine[...], theirs[...])
    high = jnp.where(first, theirs[...], mine[...])
    for core, pieces in enumerate((low, high)):
        for v in range(8):
            column = (core * 2 + v % 2) * width
            out[v // 2 * 16 : v // 2 * 16 + 16, column : column + width] = pieces[v]


IN_VMEM = pl.BlockSpec(memory_space=pltpu.VMEM)
IN_HBM = pl.BlockSpec(memory_space=pltpu.HBM)
IN_SMEM = pl.BlockSpec(memory_space=pltpu.SMEM)


def params(limit=VMEM_BYTES):
    return pltpu.CompilerParams(vmem_limit_bytes=limit)


def shards(
    student_hidden,
    student_weight,
    teacher_hidden,
    teacher_weight,
    token_ids,
    group_ids,
    response_mask,
):
    own_rows = student_hidden.shape[0]
    half = own_rows // 2
    head_rows, width = student_weight.shape
    width_t = teacher_weight.shape[1]
    tokens = token_ids.shape[0]
    dp, vocab = lax.axis_index("dp"), lax.axis_index("vocab")
    core = vocab % 2
    odd = (vocab // 4) % 2
    half_width = width // 2
    scalars = jnp.stack(first_rows(core, odd, dp // 4, dp % 4, half) + [(dp * 16 + vocab) * head_rows]).astype(I32)
    core_scalar = core.astype(I32).reshape(1)

    kept = pl.pallas_call(
        half_kernel,
        in_specs=[IN_SMEM] + [IN_HBM] * 2,
        out_specs=IN_HBM,
        out_shape=jax.ShapeDtypeStruct((half, width + width_t), BF16),
        scratch_shapes=[pltpu.VMEM((half, width + width_t), BF16), pltpu.SemaphoreType.DMA((3,))],
        compiler_params=params(),
    )((core + odd - 2 * core * odd).astype(I32).reshape(1), student_hidden, teacher_hidden)
    same_group = group_ids[:, None] == group_ids[None, :]
    lengths = jnp.sum(same_group.astype(F32), axis=1)
    token_weight = (response_mask.astype(F32) * SPAN / lengths).reshape(1, tokens)
    weight_columns = lax.dynamic_slice_in_dim(student_weight, (1 - core) * half_width, half_width, 1)
    blocks, (scalars, core_scalar, token_weight, ids, weight_columns) = gather_tokens(
        kept, (scalars, core_scalar, token_weight, token_ids.reshape(1, tokens), weight_columns)
    )

    student_logits, teacher_logits, stats, hidden = pl.pallas_call(
        functools.partial(logits_kernel, half),
        in_specs=[IN_SMEM] + [IN_VMEM] * 16 + [IN_HBM] * 2 + [IN_VMEM],
        out_specs=[IN_HBM] * 2 + [IN_VMEM, IN_HBM],
        out_shape=[
            jax.ShapeDtypeStruct((head_rows, tokens), F32),
            jax.ShapeDtypeStruct((head_rows, tokens), F32),
            jax.ShapeDtypeStruct((64, 2, 8, 128), F32),
            jax.ShapeDtypeStruct((tokens, width), BF16),
        ],
        scratch_shapes=[
            pltpu.VMEM((tokens, width), BF16),
            pltpu.VMEM((tokens, width_t), BF16),
            pltpu.VMEM((head_rows, width), BF16),
            pltpu.VMEM((head_rows, width_t), BF16),
            pltpu.VMEM((head_rows, tokens), F32),
            pltpu.VMEM((head_rows, tokens), F32),
            pltpu.SemaphoreType.DMA((2, 15)),
            pltpu.SemaphoreType.DMA((2, 5)),
        ],
        compiler_params=params(42 * 1024 * 1024),
        cost_estimate=pl.CostEstimate(
            flops=2 * head_rows * tokens * (width + width_t), bytes_accessed=24_000_000, transcendentals=2 * head_rows * tokens
        ),
    )(scalars, student_hidden, teacher_hidden, *blocks, student_weight, teacher_weight, ids)

    student_theirs, teacher_theirs, weight_columns = lax.optimization_barrier(
        (*swap([student_logits, teacher_logits]), weight_columns)
    )
    weight_theirs = send(weight_columns, OTHER_CORE)
    every = lax.all_to_all(stats.reshape(128, 8, 128), BOTH, split_axis=0, concat_axis=0, tiled=True)
    both_s, both_t = pl.pallas_call(
        join_kernel,
        in_specs=[IN_HBM] * 4,
        out_specs=[IN_HBM] * 2,
        out_shape=[jax.ShapeDtypeStruct((2 * head_rows, tokens), F32)] * 2,
        scratch_shapes=[pltpu.VMEM((2, 2 * head_rows, tokens), F32), pltpu.SemaphoreType.DMA((6,))],
        compiler_params=params(),
        cost_estimate=pl.CostEstimate(flops=0, bytes_accessed=11_000_000, transcendentals=0),
    )(student_logits, teacher_logits, student_theirs, teacher_theirs)
    every, both_s, both_t = lax.optimization_barrier((every, both_s, both_t))
    mine = pl.pallas_call(
        combine_kernel,
        in_specs=[IN_VMEM],
        out_specs=IN_VMEM,
        out_shape=jax.ShapeDtypeStruct((8, 128), F32),
        compiler_params=params(4 * 1024 * 1024),
    )(every)
    other = send(mine, OTHER_CORE)

    groups, quarter = tokens // 16, half_width // 2
    share, grad_t = pl.pallas_call(
        share_kernel,
        in_specs=[IN_SMEM] + [IN_HBM] * 2 + [IN_VMEM] + [IN_HBM] * 4,
        out_specs=[IN_HBM, IN_HBM],
        out_shape=[
            jax.ShapeDtypeStruct((groups, 2, 16, quarter), BF16),
            jax.ShapeDtypeStruct((head_rows, tokens), BF16),
        ],
        scratch_shapes=[
            pltpu.VMEM((2, 8, 128), F32),
            pltpu.VMEM((8, tokens), F32),
            pltpu.VMEM((2 * head_rows, tokens), F32),
            pltpu.VMEM((2 * head_rows, tokens), F32),
            pltpu.VMEM((tokens, 2 * head_rows), BF16),
            pltpu.VMEM((head_rows, tokens), BF16),
            pltpu.VMEM((half_width // 512, 2 * head_rows, 512), BF16),
            pltpu.VMEM((groups, 2, 16, quarter), BF16),
            pltpu.SemaphoreType.DMA((8, 10)),
        ],
        compiler_params=params(),
        cost_estimate=pl.CostEstimate(flops=2 * head_rows * tokens * width, bytes_accessed=16_000_000, transcendentals=0),
    )(
        core_scalar, mine, other, token_weight, both_s, both_t, student_weight, weight_theirs,
    )
    parts = lax.all_to_all(
        share.reshape(64, 16, quarter), BOTH, split_axis=0, concat_axis=0, tiled=True, axis_index_groups=SAME_CORE
    )

    grad_weight = pl.pallas_call(
        grad_weight_kernel,
        grid=(width // 1024,),
        in_specs=[
            pl.BlockSpec((head_rows, tokens), lambda k: (0, 0)),
            pl.BlockSpec((tokens, 1024), lambda k: (0, k)),
        ],
        out_specs=pl.BlockSpec((head_rows, 1024), lambda k: (0, k)),
        out_shape=jax.ShapeDtypeStruct((head_rows, width), BF16),
        compiler_params=params(16 * 1024 * 1024),
        cost_estimate=pl.CostEstimate(flops=2 * head_rows * tokens * width, bytes_accessed=13_000_000, transcendentals=0),
    )(grad_t, hidden)
    low, high = jnp.where(core == 0, mine, other), jnp.where(core == 0, other, mine)
    kl_all = jnp.concatenate([low[4:6], high[4:6]]).reshape(tokens)
    logp_all = jnp.concatenate([low[6:8], high[6:8]]).reshape(tokens)
    kl_tok = lax.dynamic_slice_in_dim(kl_all, dp * own_rows, own_rows, 0)
    logp_tok = lax.dynamic_slice_in_dim(logp_all, dp * own_rows, own_rows, 0)
    parts, grad_weight, kl_tok, logp_tok = lax.optimization_barrier((parts, grad_weight, kl_tok, logp_tok))

    summed = pl.pallas_call(
        sum_kernel,
        in_specs=[IN_VMEM],
        out_specs=IN_VMEM,
        out_shape=jax.ShapeDtypeStruct((8, 16, quarter), BF16),
        compiler_params=params(8 * 1024 * 1024),
    )(parts)
    pieces_mine = lax.all_to_all(
        summed,
        BOTH, split_axis=0, concat_axis=0, tiled=True, axis_index_groups=SAME_TOKENS,
    )
    pieces_theirs = send(pieces_mine, OTHER_CORE)
    grad_hidden = pl.pallas_call(
        assemble_kernel,
        in_specs=[IN_SMEM] + [IN_VMEM] * 2,
        out_specs=IN_VMEM,
        out_shape=jax.ShapeDtypeStruct((own_rows, width), BF16),
        compiler_params=params(8 * 1024 * 1024),
    )(core_scalar, pieces_mine, pieces_theirs)
    return (kl_tok, logp_tok, grad_hidden, grad_weight)


def solution(mesh):
    in_specs = (
        P("dp", None),
        P(("dp", "vocab"), None),
        P("dp", None),
        P(("dp", "vocab"), None),
        P(),
        P(),
        P(),
    )
    out_specs = (P("dp"), P("dp"), P("dp", None), P(("dp", "vocab"), None))
    return jax.shard_map(shards, mesh=mesh, in_specs=in_specs, out_specs=out_specs, check_vma=False)
```

```python
import functools

import jax
import jax.numpy as jnp
from jax import lax
from jax.experimental import pallas as pl
from jax.experimental.pallas import tpu as pltpu
from jax.sharding import PartitionSpec as P

SPAN = 32
BOTH = ("dp", "vocab")
F32 = jnp.float32
BF16 = jnp.bfloat16
I32 = jnp.int32
VMEM_BYTES = 63 * 1024 * 1024


def coordinates(device):
    dp, vocab = divmod(device, 16)
    x_lo, z = divmod(dp, 4)
    y, rest = divmod(vocab, 4)
    x_hi, core = divmod(rest, 2)
    return x_hi * 2 + x_lo, y, z, core


def device_at(x, y, z, core):
    x_hi, x_lo = divmod(x % 4, 2)
    return (x_lo * 4 + z % 4) * 16 + (y % 4) * 4 + x_hi * 2 + core


def permutation(move):
    return [(i, device_at(*move(*coordinates(i)))) for i in range(128)]


def way(core):
    return 1 - 2 * core


ALONG_Z = permutation(lambda x, y, z, c: (x, y, z + way(c), c))
ALONG_X = permutation(lambda x, y, z, c: (x + way(c), y, z, c))
ALONG_Y = permutation(lambda x, y, z, c: (x, y + way(c), z, c))
OTHER_CORE = permutation(lambda x, y, z, c: (x, y, z, 1 - c))
SAME_TOKENS = [[dp * 16 + v * 2 + c for v in range(8)] for dp in range(8) for c in range(2)]
SAME_CORE = [[i for i in range(128) if i % 2 == c] for c in range(2)]


def send(value, where):
    return lax.ppermute(value, BOTH, where)


def after(done, then):
    both = lax.optimization_barrier((done, then))
    return both


def swap(blocks):
    return [send(block, OTHER_CORE) for block in blocks]


def gather_tokens(kept, others):
    near_z, near_x, others = lax.optimization_barrier((send(kept, ALONG_Z), send(kept, ALONG_X), others))
    second = [send(near_z, ALONG_X), send(near_z, ALONG_Z), send(near_z, ALONG_Y)] + swap([near_z, near_x])
    near_zx, far_z, rest_z, o_near_z, o_near_x = lax.optimization_barrier(second)
    far_zx, rest_zx = send(far_z, ALONG_X), send(near_zx, ALONG_Y)
    far_zx, o_near_zx, o_far_z, rest_z = lax.optimization_barrier((far_zx, *swap([near_zx, far_z]), rest_z))
    o_rest_z, o_far_zx, o_rest_zx = swap([rest_z, far_zx, rest_zx])
    scalars, core_scalar, token_weight, ids, weight_columns = others
    o_rest_z, o_far_zx, o_rest_zx, weight_columns = lax.optimization_barrier((o_rest_z, o_far_zx, o_rest_zx, weight_columns))
    weight_theirs = send(weight_columns, OTHER_CORE)
    mine = [near_z, rest_z, near_x, far_z, near_zx, rest_zx, far_zx]
    theirs = [o_near_z, o_rest_z, o_near_x, o_far_z, o_near_zx, o_rest_zx, o_far_zx]
    return mine + theirs, (scalars, core_scalar, token_weight, ids, weight_theirs)


def first_rows(core, odd, x_lo, z, half):
    def block(xl, zz):
        return (xl * 4 + jnp.remainder(zz, 4)) * 2

    def arrived(c):
        s = 1 - 2 * c
        k = c + odd - 2 * c * odd
        return [
            block(x_lo, z - s) + k,
            block(x_lo, z - s) + 1 - k,
            block(1 - x_lo, z) + k,
            block(x_lo, z + 2) + k,
            block(1 - x_lo, z - s) + k,
            block(1 - x_lo, z - s) + 1 - k,
            block(1 - x_lo, z + 2) + k,
        ]

    return [half * b for b in [block(x_lo, z)] + arrived(core) + arrived(1 - core)]


def start_all(copies):
    for copy in copies:
        copy.start()
    return copies


def wait_all(copies):
    for copy in copies:
        copy.wait()


def half_kernel(scalars, student, teacher, out, here, sems):
    half, width = out.shape[0], student.shape[1]
    rows = pl.ds(pl.multiple_of(scalars[0] * half, half), half)
    loads = [
        pltpu.make_async_copy(student.at[rows], here.at[:, pl.ds(0, width)], sems.at[0]),
        pltpu.make_async_copy(teacher.at[rows], here.at[:, pl.ds(width, teacher.shape[1])], sems.at[1]),
    ]
    wait_all(start_all(loads))
    store = pltpu.make_async_copy(here, out, sems.at[2])
    store.start()
    store.wait()


def place(scalars, own, blocks, columns, hidden, half, sems):
    copies = []
    for i, block in enumerate([own] + [b.at[:, columns] for b in blocks]):
        rows = pl.ds(pl.multiple_of(scalars[i], half), own.shape[0] if i == 0 else half)
        copies.append(pltpu.make_async_copy(block, hidden.at[rows], sems.at[i]))
    return start_all(copies)


def rows_product(weight, hidden, out, at):
    out[at] = lax.dot_general(weight[at], hidden[...], (((1,), (1,)), ((), ())), preferred_element_type=F32)


def logits_kernel(half, scalars, own_s, own_t, *refs):
    blocks = refs[:14]
    weight_s, weight_t, ids, out_s, out_t, stats, out_hidden = refs[14:21]
    hidden_s, hidden_t, here_s, here_t, logits_s, logits_t, place_sems, sems = refs[21:]
    rows = out_s.shape[0] // 2
    width_s, width_t = hidden_s.shape[1], hidden_t.shape[1]
    parts = [slice(i * rows, (i + 1) * rows) for i in range(2)]
    heads = [
        (own_s, pl.ds(0, width_s), weight_s, out_s, hidden_s, here_s, logits_s),
        (own_t, pl.ds(width_s, width_t), weight_t, out_t, hidden_t, here_t, logits_t),
    ]
    placing, loads, stores = [], [], []
    for h, (own, columns, weight, out, hidden, here, logits) in enumerate(heads):
        loads.append([pltpu.make_async_copy(weight.at[at], here.at[at], sems.at[h, i]) for i, at in enumerate(parts)])
        stores.append([pltpu.make_async_copy(logits.at[at], out.at[at], sems.at[h, 2 + i]) for i, at in enumerate(parts)])

    def start_placing(h):
        own, columns, _, _, hidden, _, _ = heads[h]
        placing.append(place(scalars, own, blocks, columns, hidden, half, place_sems.at[h]))

    def product(h, i):
        _, _, _, _, hidden, here, logits = heads[h]
        rows_product(here, hidden, logits, parts[i])
        stores[h][i].start()

    tiles = [slice(j * 128, (j + 1) * 128) for j in range(out_s.shape[1] // 128)]

    def put(j, row, value):
        side, k = divmod(j, 2)
        stats[:, side, pl.ds(row * 2 + k, 1), :] = jnp.broadcast_to(value[None], (stats.shape[0], 1, 128))

    loads[0][0].start()
    start_placing(0)
    wait_all(placing[0])
    loads[0][1].start()
    loads[0][0].wait()
    start_placing(1)
    product(0, 0)
    loads[0][1].wait()
    start_all(loads[1])
    product(0, 1)
    keep = pltpu.make_async_copy(hidden_s, out_hidden, sems.at[1, 4])
    entry = lax.broadcasted_iota(I32, (out_s.shape[0], 128), 0) + scalars[15]
    for j, at in enumerate(tiles):
        s = logits_s[:, at]
        top = jnp.max(s, axis=0, keepdims=True)
        put(j, 0, top + jnp.log(jnp.sum(jnp.exp(s - top), axis=0, keepdims=True)))
        put(j, 3, jnp.sum(jnp.where(ids[:, at] == entry, s, 0.0), axis=0, keepdims=True))
    wait_all(placing[1])
    wait_all(loads[1])
    keep.start()
    for i in range(2):
        product(1, i)
    for j, at in enumerate(tiles):
        t = logits_t[:, at]
        top = jnp.max(t, axis=0, keepdims=True)
        exp_t = jnp.exp(t - top)
        total = jnp.sum(exp_t, axis=0, keepdims=True)
        put(j, 1, top + jnp.log(total))
        put(j, 2, jnp.sum(exp_t * (t - logits_s[:, at]), axis=0, keepdims=True) / total)
    wait_all(stores[0])
    wait_all(stores[1])
    keep.wait()


def combine_kernel(every, out):
    stats = every[...]
    lse = stats[:, 0:4]
    top = jnp.max(lse, axis=0)
    total = top + jnp.log(jnp.sum(jnp.exp(lse - top[None]), axis=0))
    total_s, total_t = total[0:2], total[2:4]
    cross = jnp.sum(jnp.exp(stats[:, 2:4] - total_t[None]) * stats[:, 4:6], axis=0)
    picked = jnp.sum(stats[:, 6:8], axis=0)
    out[0:4] = total
    out[4:6] = cross - total_t + total_s
    out[6:8] = picked - total_s


def join_kernel(s_mine, t_mine, s_theirs, t_theirs, s_out, t_out, here, sems):
    rows = s_mine.shape[0]
    given = ((s_mine, t_mine), (s_theirs, t_theirs))
    loads = [
        pltpu.make_async_copy(given[side][h], here.at[h, pl.ds(side * rows, rows)], sems.at[2 * h + side])
        for h in range(2)
        for side in range(2)
    ]
    stores = [pltpu.make_async_copy(here.at[h], out, sems.at[4 + h]) for h, out in enumerate((s_out, t_out))]
    start_all(loads)
    for h in range(2):
        wait_all(loads[2 * h : 2 * h + 2])
        stores[h].start()
    wait_all(stores)


def share_kernel(
    scalars, mine, other, factor, student, teacher, weight_mine, weight_theirs, share, out_t,
    small, totals, s_here, t_here, grad, grad_t, weight, part, sems,
):
    rows, width = weight_theirs.shape
    tokens = student.shape[1]
    tile = weight.shape[2]
    steps = width // tile
    count = rows // 128
    figures = start_all(
        [pltpu.make_async_copy(mine, small.at[0], sems.at[4, 2]), pltpu.make_async_copy(other, small.at[1], sems.at[4, 3])]
    )
    logits = []
    for j in range(2 * count):
        at = pl.ds(j * 128, 128)
        logits.append(
            start_all(
                [
                    pltpu.make_async_copy(student.at[at], s_here.at[at], sems.at[0, j]),
                    pltpu.make_async_copy(teacher.at[at], t_here.at[at], sems.at[1, j]),
                ]
            )
        )
    waiting = []

    def load_weight():
        k = len(waiting)
        if k == steps:
            return
        columns = pl.ds(pl.multiple_of(scalars[0] * width + k * tile, 128), tile)
        waiting.append(
            start_all(
                [
                    pltpu.make_async_copy(weight_mine.at[:, columns], weight.at[k, pl.ds(0, rows)], sems.at[5, k]),
                    pltpu.make_async_copy(
                        weight_theirs.at[:, pl.ds(k * tile, tile)], weight.at[k, pl.ds(rows, rows)], sems.at[6, k]
                    ),
                ]
            )
        )

    load_weight()
    first = scalars[0] == 0
    wait_all(figures)
    low, high = jnp.where(first, small[0], small[1]), jnp.where(first, small[1], small[0])
    for j in range(tokens // 128):
        half, k = (low, high)[j // 2], j % 2
        for i in range(2):
            totals[i : i + 1, j * 128 : (j + 1) * 128] = half[2 * i + k : 2 * i + k + 1]
    stores = []
    for i, pair in enumerate(logits):
        wait_all(pair)
        at = slice(i * 128, (i + 1) * 128)
        value = factor[...] * (jnp.exp(s_here[at] - totals[0:1]) - jnp.exp(t_here[at] - totals[1:2]))
        if i < count:
            grad_t[at] = value.astype(BF16)
            stores.append(pltpu.make_async_copy(grad_t.at[pl.ds(i * 128, 128)], out_t.at[pl.ds(i * 128, 128)], sems.at[7, i]))
            stores[-1].start()
        grad[:, at] = value.T.astype(BF16)
        if i in (count - 1, 2 * count - 3):
            load_weight()
    written = 0
    for k in range(steps):
        wait_all(waiting[k])
        load_weight()
        product = jnp.dot(grad[...], weight[k], preferred_element_type=F32).astype(BF16)
        for j in range(tile // 256):
            high_at, low_at = divmod(k * tile + j * 256, share.shape[3])
            part[:, high_at, :, pl.ds(low_at, 256)] = product[:, j * 256 : (j + 1) * 256].reshape(share.shape[0], 16, 256)
        while (k + 1) * tile >= (written + 1) * share.shape[3]:
            stores.append(pltpu.make_async_copy(part.at[:, written], share.at[:, written], sems.at[4, written]))
            stores[-1].start()
            written += 1
    wait_all(stores)


def grad_weight_kernel(grad, hidden, out):
    out[...] = jnp.dot(grad[...], hidden[...], preferred_element_type=F32).astype(BF16)


def sum_kernel(parts, out):
    count = parts.shape[0] // 16
    total = jnp.sum(parts[0:count].astype(F32), axis=0)
    for i in range(1, 16):
        total += jnp.sum(parts[count * i : count * (i + 1)].astype(F32), axis=0)
    out[...] = jnp.broadcast_to(total.astype(BF16)[None], out.shape)


def assemble_kernel(scalars, mine, theirs, out):
    width = mine.shape[2]
    first = scalars[0] == 0
    low = jnp.where(first, mine[...], theirs[...])
    high = jnp.where(first, theirs[...], mine[...])
    for core, pieces in enumerate((low, high)):
        for v in range(8):
            column = (core * 2 + v % 2) * width
            out[v // 2 * 16 : v // 2 * 16 + 16, column : column + width] = pieces[v]


IN_VMEM = pl.BlockSpec(memory_space=pltpu.VMEM)
IN_HBM = pl.BlockSpec(memory_space=pltpu.HBM)
IN_SMEM = pl.BlockSpec(memory_space=pltpu.SMEM)


def params(limit=VMEM_BYTES):
    return pltpu.CompilerParams(vmem_limit_bytes=limit)


def shards(
    student_hidden,
    student_weight,
    teacher_hidden,
    teacher_weight,
    token_ids,
    group_ids,
    response_mask,
):
    own_rows = student_hidden.shape[0]
    half = own_rows // 2
    head_rows, width = student_weight.shape
    width_t = teacher_weight.shape[1]
    tokens = token_ids.shape[0]
    dp, vocab = lax.axis_index("dp"), lax.axis_index("vocab")
    core = vocab % 2
    odd = (vocab // 4) % 2
    half_width = width // 2
    scalars = jnp.stack(first_rows(core, odd, dp // 4, dp % 4, half) + [(dp * 16 + vocab) * head_rows]).astype(I32)
    core_scalar = core.astype(I32).reshape(1)

    kept = pl.pallas_call(
        half_kernel,
        in_specs=[IN_SMEM] + [IN_HBM] * 2,
        out_specs=IN_HBM,
        out_shape=jax.ShapeDtypeStruct((half, width + width_t), BF16),
        scratch_shapes=[pltpu.VMEM((half, width + width_t), BF16), pltpu.SemaphoreType.DMA((3,))],
        compiler_params=params(),
    )((core + odd - 2 * core * odd).astype(I32).reshape(1), student_hidden, teacher_hidden)
    same_group = group_ids[:, None] == group_ids[None, :]
    lengths = jnp.sum(same_group.astype(F32), axis=1)
    token_weight = (response_mask.astype(F32) * SPAN / lengths).reshape(1, tokens)
    weight_columns = lax.dynamic_slice_in_dim(student_weight, (1 - core) * half_width, half_width, 1)
    blocks, (scalars, core_scalar, token_weight, ids, weight_theirs) = gather_tokens(
        kept, (scalars, core_scalar, token_weight, token_ids.reshape(1, tokens), weight_columns)
    )

    student_logits, teacher_logits, stats, hidden = pl.pallas_call(
        functools.partial(logits_kernel, half),
        in_specs=[IN_SMEM] + [IN_VMEM] * 16 + [IN_HBM] * 2 + [IN_VMEM],
        out_specs=[IN_HBM] * 2 + [IN_VMEM, IN_HBM],
        out_shape=[
            jax.ShapeDtypeStruct((head_rows, tokens), F32),
            jax.ShapeDtypeStruct((head_rows, tokens), F32),
            jax.ShapeDtypeStruct((64, 2, 8, 128), F32),
            jax.ShapeDtypeStruct((tokens, width), BF16),
        ],
        scratch_shapes=[
            pltpu.VMEM((tokens, width), BF16),
            pltpu.VMEM((tokens, width_t), BF16),
            pltpu.VMEM((head_rows, width), BF16),
            pltpu.VMEM((head_rows, width_t), BF16),
            pltpu.VMEM((head_rows, tokens), F32),
            pltpu.VMEM((head_rows, tokens), F32),
            pltpu.SemaphoreType.DMA((2, 15)),
            pltpu.SemaphoreType.DMA((2, 5)),
        ],
        compiler_params=params(42 * 1024 * 1024),
        cost_estimate=pl.CostEstimate(
            flops=2 * head_rows * tokens * (width + width_t), bytes_accessed=24_000_000, transcendentals=2 * head_rows * tokens
        ),
    )(scalars, student_hidden, teacher_hidden, *blocks, student_weight, teacher_weight, ids)

    student_theirs, teacher_theirs = swap([student_logits, teacher_logits])
    every = lax.all_to_all(stats.reshape(128, 8, 128), BOTH, split_axis=0, concat_axis=0, tiled=True)
    both_s, both_t = pl.pallas_call(
        join_kernel,
        in_specs=[IN_HBM] * 4,
        out_specs=[IN_HBM] * 2,
        out_shape=[jax.ShapeDtypeStruct((2 * head_rows, tokens), F32)] * 2,
        scratch_shapes=[pltpu.VMEM((2, 2 * head_rows, tokens), F32), pltpu.SemaphoreType.DMA((6,))],
        compiler_params=params(),
        cost_estimate=pl.CostEstimate(flops=0, bytes_accessed=11_000_000, transcendentals=0),
    )(student_logits, teacher_logits, student_theirs, teacher_theirs)
    every, both_s, both_t = lax.optimization_barrier((every, both_s, both_t))
    mine = pl.pallas_call(
        combine_kernel,
        in_specs=[IN_VMEM],
        out_specs=IN_VMEM,
        out_shape=jax.ShapeDtypeStruct((8, 128), F32),
        compiler_params=params(4 * 1024 * 1024),
    )(every)
    other = send(mine, OTHER_CORE)

    groups, quarter = tokens // 16, half_width // 2
    share, grad_t = pl.pallas_call(
        share_kernel,
        in_specs=[IN_SMEM] + [IN_HBM] * 2 + [IN_VMEM] + [IN_HBM] * 4,
        out_specs=[IN_HBM, IN_HBM],
        out_shape=[
            jax.ShapeDtypeStruct((groups, 2, 16, quarter), BF16),
            jax.ShapeDtypeStruct((head_rows, tokens), BF16),
        ],
        scratch_shapes=[
            pltpu.VMEM((2, 8, 128), F32),
            pltpu.VMEM((8, tokens), F32),
            pltpu.VMEM((2 * head_rows, tokens), F32),
            pltpu.VMEM((2 * head_rows, tokens), F32),
            pltpu.VMEM((tokens, 2 * head_rows), BF16),
            pltpu.VMEM((head_rows, tokens), BF16),
            pltpu.VMEM((half_width // 512, 2 * head_rows, 512), BF16),
            pltpu.VMEM((groups, 2, 16, quarter), BF16),
            pltpu.SemaphoreType.DMA((8, 10)),
        ],
        compiler_params=params(),
        cost_estimate=pl.CostEstimate(flops=2 * head_rows * tokens * width, bytes_accessed=16_000_000, transcendentals=0),
    )(
        core_scalar, mine, other, token_weight, both_s, both_t, student_weight, weight_theirs,
    )
    parts = lax.all_to_all(
        share.reshape(64, 16, quarter), BOTH, split_axis=0, concat_axis=0, tiled=True, axis_index_groups=SAME_CORE
    )

    grad_weight = pl.pallas_call(
        grad_weight_kernel,
        grid=(width // 1024,),
        in_specs=[
            pl.BlockSpec((head_rows, tokens), lambda k: (0, 0)),
            pl.BlockSpec((tokens, 1024), lambda k: (0, k)),
        ],
        out_specs=pl.BlockSpec((head_rows, 1024), lambda k: (0, k)),
        out_shape=jax.ShapeDtypeStruct((head_rows, width), BF16),
        compiler_params=params(16 * 1024 * 1024),
        cost_estimate=pl.CostEstimate(flops=2 * head_rows * tokens * width, bytes_accessed=13_000_000, transcendentals=0),
    )(grad_t, hidden)
    low, high = jnp.where(core == 0, mine, other), jnp.where(core == 0, other, mine)
    kl_all = jnp.concatenate([low[4:6], high[4:6]]).reshape(tokens)
    logp_all = jnp.concatenate([low[6:8], high[6:8]]).reshape(tokens)
    kl_tok = lax.dynamic_slice_in_dim(kl_all, dp * own_rows, own_rows, 0)
    logp_tok = lax.dynamic_slice_in_dim(logp_all, dp * own_rows, own_rows, 0)
    parts, grad_weight, kl_tok, logp_tok = lax.optimization_barrier((parts, grad_weight, kl_tok, logp_tok))

    summed = pl.pallas_call(
        sum_kernel,
        in_specs=[IN_VMEM],
        out_specs=IN_VMEM,
        out_shape=jax.ShapeDtypeStruct((8, 16, quarter), BF16),
        compiler_params=params(8 * 1024 * 1024),
    )(parts)
    pieces_mine = lax.all_to_all(
        summed,
        BOTH, split_axis=0, concat_axis=0, tiled=True, axis_index_groups=SAME_TOKENS,
    )
    pieces_theirs = send(pieces_mine, OTHER_CORE)
    grad_hidden = pl.pallas_call(
        assemble_kernel,
        in_specs=[IN_SMEM] + [IN_VMEM] * 2,
        out_specs=IN_VMEM,
        out_shape=jax.ShapeDtypeStruct((own_rows, width), BF16),
        compiler_params=params(8 * 1024 * 1024),
    )(core_scalar, pieces_mine, pieces_theirs)
    return (kl_tok, logp_tok, grad_hidden, grad_weight)


def solution(mesh):
    in_specs = (
        P("dp", None),
        P(("dp", "vocab"), None),
        P("dp", None),
        P(("dp", "vocab"), None),
        P(),
        P(),
        P(),
    )
    out_specs = (P("dp"), P("dp"), P("dp", None), P(("dp", "vocab"), None))
    return jax.shard_map(shards, mesh=mesh, in_specs=in_specs, out_specs=out_specs, check_vma=False)
```
